32 devices in a mesh: depth: 4 (over x, core), tile: 8 (over z, y).
Axes of the slice: x: 2, y: 2, z: 4, core: 2. Of those that a mesh axis runs over, the one named last changes fastest.
Arguments:
- transmission: float32 [8, 2, 2048, 512], P('depth', None, 'tile'), may hold values from -5 to 5
- probe_field: float32 [2, 256, 256], replicated, may hold values from -5 to 5
- scan_positions: int32 [32, 2], P('tile'), may hold values from 0 to 1792, as said below
- amplitudes: float32 [32, 256, 256], P('tile'), may hold values from 0 to 3
Outputs:
- object_grad: float32 [8, 2, 2048, 512], P('depth', None, 'tile')
- probe_grad: float32 [2, 256, 256], P(None, 'depth')
The draws below stay inside these ranges and needn't reach their ends.
Inputs may be any that keep to these rules, and one draw needn't show every extreme that they name: `scan_positions`: column 0 holds a window's first row and column 1 its first column. The first row of window b lies in strip b // 4, that is between (b // 4) * 256 and (b // 4 + 1) * 256 - 1; windows of the last strip end inside the object, and a window's first column is at most 256.
All inputs are finite; a program needn't handle non-finite values.
Results may differ from the reference program's by a relative error of at most 0.0003.
Values sent between devices are 32-bit elements; how exact they have to be, the bound alone decides.
No kernel may reach another device: no remote copies, remote signals or barrier semaphores. Data moves between devices by JAX's collectives and lax.ppermute only.
A program may use at most 128 MiB of HBM per device.

```python
import jax
import jax.numpy as jnp
from jax import lax

W = 256
TR = 256
NCOL = 512
WIN_TILE = 4
SLICES = 8
NROWS = 2048
NWIN = 32


def draw_scan_positions(key, part):
    row_key, col_key = jax.random.split(jax.random.fold_in(key, 17))
    window_ids = jnp.arange(NWIN, dtype=jnp.int32)
    strip_ids = window_ids // WIN_TILE
    last_strip = NWIN // WIN_TILE - 1
    row_span = jnp.where(strip_ids == last_strip, TR - W + 1, TR)
    row_offsets = jax.random.randint(row_key, (NWIN,), 0, 1 << 20, dtype=jnp.int32) % row_span
    col_offsets = jax.random.randint(col_key, (NWIN,), 0, NCOL - W + 1, dtype=jnp.int32)
    row_offsets = row_offsets.at[0].set(0).at[NWIN - 1].set(TR - W)
    col_offsets = col_offsets.at[0].set(0).at[NWIN - 1].set(NCOL - W)
    return jnp.stack([strip_ids * TR + row_offsets, col_offsets], axis=1).astype(jnp.int32)


def steps_of(rng, extent, cuts, smallest, largest):
    def one(axis_at, shards_of):
        steps = jax.random.uniform(jax.random.fold_in(jax.random.fold_in(rng, 6), axis_at), (shards_of,), jnp.float32, smallest / len(cuts), largest / len(cuts))
        return jnp.repeat(jnp.exp(steps), extent[axis_at] // shards_of).reshape((-1,) + (1,) * (len(extent) - axis_at - 1))

    loudness = one(*cuts[0])
    for cut in cuts[1:]:
        loudness = loudness * one(*cut)
    return loudness


def centred(stream_key, extent, scale, limit, cuts=(), kind=jnp.bfloat16):
    factor_of = steps_of(stream_key, extent, cuts, -0.22, 0.18) if cuts else 1.0
    result = jax.random.normal(stream_key, extent, jnp.float32) * scale * factor_of
    return jnp.minimum(jnp.maximum(result, -limit), limit).astype(kind)


def setup_inputs(seed: int = 0) -> dict:
    key_list = jax.random.split(jax.random.key(seed), 5)
    return {
        "transmission": centred(key_list[0], (SLICES, 2, NROWS, NCOL), 0.71, 5.0, ((0, 4), (2, 8)), jnp.float32),
        "probe_field": centred(key_list[1], (2, W, W), 0.71, 5.0, (), jnp.float32),
        "scan_positions": draw_scan_positions(jax.random.fold_in(key_list[4], 71), 0),
        "amplitudes": jnp.clip(3.0 * jax.random.uniform(key_list[3], (NWIN, W, W), jnp.float32) ** steps_of(key_list[3], (NWIN, W, W), ((0, 8),), -0.2, 0.2), 0.0, 3.0),
    }


def fresnel_kernel(length):
    indices = jnp.arange(length, dtype=jnp.int32)
    frequency = jnp.where(indices < length // 2, indices, indices - length).astype(jnp.float32)
    phase_angle = jnp.pi * frequency * frequency / (4.0 * length)
    factor_one = lax.complex(jnp.cos(phase_angle), -jnp.sin(phase_angle))
    return factor_one[:, None] * factor_one[None, :]

def reference(transmission, probe_field, scan_positions, amplitudes):
    kernel = fresnel_kernel(W)
    anchor = jnp.zeros((), jnp.int32)

    def one_window(carry_state, window_data):
        grad_total, probe_total = carry_state
        position, measured = window_data
        corner = (anchor, anchor, position[0].astype(jnp.int32), position[1].astype(jnp.int32))
        cropped = lax.dynamic_slice(transmission, corner, (SLICES, 2, W, W))
        trans_slices = lax.complex(cropped[:, 0], cropped[:, 1])
        wave_now = lax.complex(probe_field[0], probe_field[1])
        history = []
        for layer_index in range(SLICES):
            history.append(wave_now)
            wave_now = jnp.fft.ifft2(kernel * jnp.fft.fft2(trans_slices[layer_index] * wave_now))
        far_wave = jnp.fft.fft2(wave_now, norm='ortho')
        modulus = jnp.sqrt(jnp.real(far_wave) ** 2 + jnp.imag(far_wave) ** 2 + 1.0)
        grad_wave = jnp.fft.ifft2((1.0 - measured / modulus) * far_wave, norm='ortho')
        pieces = [None] * SLICES
        for layer_index in reversed(range(SLICES)):
            back_wave = jnp.fft.ifft2(jnp.conj(kernel) * jnp.fft.fft2(grad_wave))
            pieces[layer_index] = jnp.conj(history[layer_index]) * back_wave
            grad_wave = jnp.conj(trans_slices[layer_index]) * back_wave
        stacked = jnp.stack(pieces)
        update = jnp.stack([jnp.real(stacked), jnp.imag(stacked)], axis=1)
        current = lax.dynamic_slice(grad_total, corner, (SLICES, 2, W, W))
        grad_total = lax.dynamic_update_slice(grad_total, current + update, corner)
        probe_total = probe_total + jnp.stack([jnp.real(grad_wave), jnp.imag(grad_wave)])
        return ((grad_total, probe_total), None)
    start_state = (jnp.zeros_like(transmission), jnp.zeros_like(probe_field))
    (object_grad, probe_grad), unused = lax.scan(one_window, start_state, (scan_positions, amplitudes))
    return (object_grad, probe_grad)
```

```python
import functools

import jax
import jax.numpy as jnp
import ml_dtypes
import numpy as np
from jax import lax
from jax.experimental import pallas as pl
from jax.experimental.pallas import tpu as pltpu
from jax.sharding import PartitionSpec as P

LANES = 128
VMEM_BYTES = 48 * 1024 * 1024
F32 = jnp.float32
BF16 = jnp.bfloat16


def split_table(table):
    high = table.astype(np.float32).astype(ml_dtypes.bfloat16)
    low = (table - high.astype(np.float64)).astype(np.float32).astype(ml_dtypes.bfloat16)
    return high, low


def left_form(matrix):
    return np.block([[matrix.real, -matrix.imag], [matrix.imag, matrix.real]])


def folded(matrix):
    half = matrix.shape[0] // 2
    near = matrix[:half, :half]
    mirrored = matrix[:half, half:][:, ::-1]
    return (near + mirrored) / 2, (near - mirrored) / 2


def optics_tables(length):
    index = np.arange(length)
    fourier = np.exp(-2j * np.pi * (index[:, None] * index[None, :] % length) / length)
    frequency = np.where(index < length // 2, index, index - length).astype(np.float64)
    phase = np.exp(-1j * np.pi * frequency**2 / (4 * length))
    fresnel = (np.conj(fourier) * phase[None, :]) @ fourier / length
    odd = 2 * index + 1
    turn = odd[:, None] * odd[None, :] % (4 * length)
    shifted = np.exp(-2j * np.pi * turn / (4 * length)) / np.sqrt(length)
    left, right = [], []
    for matrix in (fresnel, shifted):
        for block in folded(matrix):
            high, low = split_table(left_form(block))
            left.append(np.concatenate([high, high, low], axis=1))
            high, low = split_table(left_form(np.conj(block)))
            left.append(np.concatenate([high, high, low], axis=1))
            high, low = split_table(left_form(np.conj(block)))
            right.append(np.concatenate([high, high, low], axis=0))
            high, low = split_table(left_form(block))
            right.append(np.concatenate([high, high, low], axis=0))
    order = np.concatenate([index[: length // 2], index[length // 2 :][::-1]])
    ramp = np.exp(1j * np.pi * order / length)
    tilt = ramp[:, None] * ramp[None, :]
    return np.stack(left), np.stack(right), np.stack([tilt.real, tilt.imag]).astype(np.float32)


def reversal(size):
    row = lax.broadcasted_iota(jnp.int32, (size, size), 0)
    col = lax.broadcasted_iota(jnp.int32, (size, size), 1)
    return jnp.where(row + col == size - 1, 1.0, 0.0).astype(F32)


def exact_dot(a, b):
    return jnp.dot(a, b, precision=lax.Precision.HIGHEST, preferred_element_type=F32)


def mirror_halves(x, flip):
    half = x.shape[0] // 2
    x = jnp.concatenate([x[:, :half], exact_dot(x[:, half:], flip)], axis=1)
    return jnp.concatenate([x[:half], exact_dot(flip, x[half:])], axis=0)


def prep_kernel(ids, probe, amplitudes, probe_out, amp_out):
    flip = reversal(probe.shape[-1] // 2)
    for part in range(2):
        probe_out[part] = mirror_halves(probe[part], flip)
    amp_out[...] = mirror_halves(amplitudes[ids[0]], flip)


def crop_kernel(peers, ids, positions, own, rim, *rest):
    outs, ext = rest[:peers], rest[peers]
    planes, rows, cols = own.shape
    blocks = cols // LANES
    size = outs[0].shape[-1]
    flip = reversal(size // 2)
    lane = lax.broadcasted_iota(jnp.int32, (size, LANES), 1)
    ext[blocks] = jnp.zeros((2 * rows, LANES), F32)
    for plane in range(planes):
        for block in range(blocks):
            ext[block, 0:rows, :] = own[plane, :, block * LANES : (block + 1) * LANES]
            ext[block, rows : 2 * rows, :] = rim[plane, :, block * LANES : (block + 1) * LANES]
        for offset in range(peers):
            window = ids[0] ^ offset
            row_first = positions[window, 0] - ids[1] * rows
            col_first = positions[window, 1]
            block_first = col_first >> 7
            within = col_first & (LANES - 1)
            moved = [
                pltpu.roll(ext[block_first + i, pl.ds(row_first, size), :], (LANES - within) & (LANES - 1), 1)
                for i in range(size // LANES + 1)
            ]
            keep = lane < LANES - within
            picked = [jnp.where(keep, moved[i], moved[i + 1]) for i in range(size // LANES)]
            outs[offset][plane] = mirror_halves(jnp.concatenate(picked, axis=1), flip)


def place_kernel(peers, ids, positions, *rest):
    pieces, own, rim, ext = rest[:peers], rest[peers], rest[peers + 1], rest[peers + 2]
    planes, rows, cols = own.shape
    blocks = cols // LANES
    size = pieces[0].shape[-1]
    flip = reversal(size // 2)
    lane = lax.broadcasted_iota(jnp.int32, (size, LANES), 1)
    for plane in range(planes):
        ext[...] = jnp.zeros(ext.shape, F32)
        for offset in range(peers):
            window = ids[0] ^ offset
            row_first = positions[window, 0] - ids[1] * rows
            col_first = positions[window, 1]
            block_first = col_first >> 7
            within = col_first & (LANES - 1)
            plain = mirror_halves(pieces[offset][plane], flip)
            moved = [
                pltpu.roll(plain[:, i * LANES : (i + 1) * LANES], within, 1) for i in range(size // LANES)
            ]
            keep = lane >= within
            zero = jnp.zeros((size, LANES), F32)
            moved = [zero] + moved + [zero]
            for i in range(size // LANES + 1):
                place = (block_first + i, pl.ds(row_first, size))
                ext[place] = ext[place] + jnp.where(keep, moved[i + 1], moved[i])
        for block in range(blocks):
            own[plane, :, block * LANES : (block + 1) * LANES] = ext[block, 0:rows, :]
            rim[plane, :, block * LANES : (block + 1) * LANES] = ext[block, rows : 2 * rows, :]


def split_value(x):
    high = x.astype(BF16)
    low = (x - high.astype(F32)).astype(BF16)
    return high, low


def sandwich(re, im, left, right, base, conj):
    half = re.shape[0] // 2

    def fold(x):
        upper, lower = x[:half], x[half:]
        even, odd = upper + lower, upper - lower
        parts = []
        for y in (even, odd):
            near, far = y[:, :half], y[:, half:]
            parts.append((near + far, near - far))
        return parts

    re_parts, im_parts = fold(re), fold(im)
    middle = []
    for b in range(2):
        field = jnp.concatenate(
            [jnp.concatenate([re_parts[a][b], im_parts[a][b]], axis=1) for a in range(2)], axis=0
        )
        high, low = split_value(field)
        middle.append(
            jnp.dot(
                jnp.concatenate([high, low, high], axis=1),
                right[base + 2 * b + conj],
                preferred_element_type=F32,
            )
        )
    done = []
    for a in range(2):
        rows = slice(a * half, (a + 1) * half)
        field = jnp.concatenate(
            [
                jnp.concatenate([middle[b][rows, :half] for b in range(2)], axis=1),
                jnp.concatenate([middle[b][rows, half:] for b in range(2)], axis=1),
            ],
            axis=0,
        )
        high, low = split_value(field)
        done.append(
            jnp.dot(
                left[base + 2 * a + conj],
                jnp.concatenate([high, low, high], axis=0),
                preferred_element_type=F32,
            )
        )

    def unfold(even, odd):
        rows = jnp.concatenate([even + odd, even - odd], axis=0)
        near, far = rows[:, :half], rows[:, half:]
        return jnp.concatenate([near + far, near - far], axis=1)

    return (
        unfold(done[0][:half], done[1][:half]),
        unfold(done[0][half:], done[1][half:]),
    )


def optics_kernel(peers, per_device, ids, probe, amplitude, left, right, tilt, *rest):
    chunks = 2 * per_device
    crops = rest[: chunks * peers]
    pieces = rest[chunks * peers : 2 * chunks * peers]
    shares = rest[2 * chunks * peers : 2 * chunks * peers + peers]
    trans, history, terms, grad, copied = rest[2 * chunks * peers + peers :]
    layers = peers * per_device
    me = ids[0]
    arrivals = []
    for j in range(per_device):
        for part in range(2):
            for offset in range(peers):
                at = (me ^ offset) * per_device + j
                arrivals.append(
                    pltpu.make_async_copy(
                        crops[(j * 2 + part) * peers + offset].at[0],
                        trans.at[at, part],
                        copied.at[(j * 2 + part) * peers + offset],
                    )
                )
    for copy in arrivals:
        copy.start()
    history[0] = probe[...]
    for copy in arrivals:
        copy.wait()

    def mixed(layer):
        t_re, t_im = trans[layer, 0], trans[layer, 1]
        w_re, w_im = history[layer, 0], history[layer, 1]
        return t_re * w_re - t_im * w_im, t_re * w_im + t_im * w_re

    def forward(layer, carry):
        re, im = mixed(layer)
        re, im = sandwich(re, im, left, right, 0, 0)
        history[layer + 1, 0] = re
        history[layer + 1, 1] = im
        return carry

    lax.fori_loop(0, layers - 1, forward, 0)
    re, im = mixed(layers - 1)
    d_re, d_im = tilt[0], tilt[1]
    re, im = re * d_re - im * d_im, re * d_im + im * d_re
    re, im = sandwich(re, im, left, right, 4, 0)
    factor = 1.0 - amplitude[...] / jnp.sqrt(re * re + im * im + 1.0)
    re, im = sandwich(re * factor, im * factor, left, right, 4, 1)
    back_re, back_im = re * d_re + im * d_im, im * d_re - re * d_im

    def collect(layer, back_re, back_im):
        w_re, w_im = history[layer, 0], history[layer, 1]
        terms[layer, 0] = w_re * back_re + w_im * back_im
        terms[layer, 1] = w_re * back_im - w_im * back_re
        t_re, t_im = trans[layer, 0], trans[layer, 1]
        grad[0] = t_re * back_re + t_im * back_im
        grad[1] = t_re * back_im - t_im * back_re

    collect(layers - 1, back_re, back_im)

    def backward(step, carry):
        back_re, back_im = sandwich(grad[0], grad[1], left, right, 0, 1)
        collect(layers - 2 - step, back_re, back_im)
        return carry

    lax.fori_loop(0, layers - 1, backward, 0)
    departures = []
    for j in range(per_device):
        for part in range(2):
            for offset in range(peers):
                at = (me ^ offset) * per_device + j
                departures.append(
                    pltpu.make_async_copy(
                        terms.at[at, part],
                        pieces[(j * 2 + part) * peers + offset].at[0],
                        copied.at[(j * 2 + part) * peers + offset],
                    )
                )
    for copy in departures:
        copy.start()
    flip = reversal(grad.shape[-1] // 2)
    share_rows = shares[0].shape[1]
    for part in range(2):
        grad[part] = mirror_halves(grad[part], flip)
    for offset in range(peers):
        first = pl.multiple_of((me ^ offset) * share_rows, share_rows)
        shares[offset][...] = grad[:, pl.ds(first, share_rows), :]
    for copy in departures:
        copy.wait()


SMEM_SPEC = pl.BlockSpec(memory_space=pltpu.SMEM)
VMEM_SPEC = pl.BlockSpec(memory_space=pltpu.VMEM)
ANY_SPEC = pl.BlockSpec(memory_space=pl.ANY)


def run_kernel(kernel, name, out_shapes, in_specs, out_specs, scratch, micros):
    return pl.pallas_call(
        kernel,
        name=name,
        out_shape=out_shapes,
        in_specs=in_specs,
        out_specs=out_specs,
        scratch_shapes=scratch,
        compiler_params=pltpu.CompilerParams(vmem_limit_bytes=VMEM_BYTES),
        cost_estimate=pl.CostEstimate(
            flops=int(micros * 1e9), bytes_accessed=int(micros * 1e6), transcendentals=0
        ),
    )


def shape(*dims):
    return jax.ShapeDtypeStruct(dims, F32)


def swap(x, axis, offset):
    peers = lax.axis_size(axis)
    return lax.ppermute(x, axis, [(i, i ^ offset) for i in range(peers)])


def shift(x, axis, by):
    peers = lax.axis_size(axis)
    return lax.ppermute(x, axis, [(i, i + by) for i in range(peers) if 0 <= i + by < peers])


def body(transmission, probe_field, scan_positions, amplitudes):
    size = probe_field.shape[-1]
    per_device, _, rows, cols = transmission.shape
    peers = lax.axis_size("depth")
    tiles = lax.axis_size("tile")
    ids = jnp.stack([lax.axis_index("depth"), lax.axis_index("tile")]).astype(jnp.int32)
    left, right, tilt = (jnp.asarray(x) for x in optics_tables(size))

    probe, amplitude = run_kernel(
        prep_kernel,
        "prep",
        (shape(2, size, size), shape(size, size)),
        [SMEM_SPEC, VMEM_SPEC, VMEM_SPEC],
        [VMEM_SPEC, VMEM_SPEC],
        [],
        2,
    )(ids, probe_field, amplitudes)

    chunks = [(j, part) for j in range(per_device) for part in range(2)]
    strips = {c: transmission[c[0], c[1]][None] for c in chunks}
    rims = {c: shift(strips[c], "tile", -1) for c in chunks}
    crops = {}
    for c in chunks:
        mine = run_kernel(
            functools.partial(crop_kernel, peers),
            "crop",
            (shape(1, size, size),) * peers,
            [SMEM_SPEC, SMEM_SPEC, VMEM_SPEC, VMEM_SPEC],
            [VMEM_SPEC] * peers,
            [pltpu.VMEM((cols // LANES + 1, 2 * rows, LANES), F32)],
            2,
        )(ids, scan_positions, strips[c], rims[c])
        crops[c] = [mine[0]] + [swap(mine[m], "depth", m) for m in range(1, peers)]

    layers = per_device * peers
    result = run_kernel(
        functools.partial(optics_kernel, peers, per_device),
        "optics",
        (shape(1, size, size),) * (len(chunks) * peers) + (shape(2, size // peers, size),) * peers,
        [SMEM_SPEC, VMEM_SPEC, VMEM_SPEC, VMEM_SPEC, VMEM_SPEC, VMEM_SPEC] + [ANY_SPEC] * (len(chunks) * peers),
        [ANY_SPEC] * (len(chunks) * peers) + [VMEM_SPEC] * peers,
        [
            pltpu.VMEM((layers, 2, size, size), F32),
            pltpu.VMEM((layers, 2, size, size), F32),
            pltpu.VMEM((layers, 2, size, size), F32),
            pltpu.VMEM((2, size, size), F32),
            pltpu.SemaphoreType.DMA((len(chunks) * peers,)),
        ],
        20,
    )(ids, probe, amplitude, left, right, tilt, *[x for c in chunks for x in crops[c]])

    own, rim_back = {}, {}
    for c in reversed(chunks):
        at = chunks.index(c) * peers
        mine = result[at : at + peers]
        returned = [mine[0]] + [swap(mine[m], "depth", m) for m in range(1, peers)]
        own[c], outside = run_kernel(
            functools.partial(place_kernel, peers),
            "place",
            (shape(1, rows, cols), shape(1, rows, cols)),
            [SMEM_SPEC, SMEM_SPEC] + [VMEM_SPEC] * peers,
            [VMEM_SPEC, VMEM_SPEC],
            [pltpu.VMEM((cols // LANES + 1, 2 * rows, LANES), F32)],
            2,
        )(ids, scan_positions, *returned)
        rim_back[c] = shift(outside, "tile", 1)

    shares = result[len(chunks) * peers :]
    probe_grad = shares[0]
    for m in range(1, peers):
        probe_grad = probe_grad + swap(shares[m], "depth", m)
    step = 1
    while step < tiles:
        probe_grad = probe_grad + swap(probe_grad, "tile", step)
        step *= 2
    object_grad = jnp.stack(
        [
            jnp.stack([own[(j, part)][0] + rim_back[(j, part)][0] for part in range(2)])
            for j in range(per_device)
        ]
    )
    return (object_grad, probe_grad)


def solution(mesh):
    placed = (P("depth", None, "tile", None), P(), P("tile", None), P("tile", None, None))
    return jax.shard_map(
        body,
        mesh=mesh,
        in_specs=placed,
        out_specs=(P("depth", None, "tile", None), P(None, "depth", None)),
        check_vma=False,
    )
```

```python
import functools

import jax
import jax.numpy as jnp
import ml_dtypes
import numpy as np
from jax import lax
from jax.experimental import pallas as pl
from jax.experimental.pallas import tpu as pltpu
from jax.sharding import PartitionSpec as P

LANES = 128
F32 = jnp.float32
BF16 = jnp.bfloat16


def split_table(table):
    high = table.astype(np.float32).astype(ml_dtypes.bfloat16)
    low = (table - high.astype(np.float64)).astype(np.float32).astype(ml_dtypes.bfloat16)
    return high, low


def left_form(matrix):
    return np.block([[matrix.real, -matrix.imag], [matrix.imag, matrix.real]])


def folded(matrix):
    half = matrix.shape[0] // 2
    near = matrix[:half, :half]
    mirrored = matrix[:half, half:][:, ::-1]
    return (near + mirrored) / 2, (near - mirrored) / 2


def optics_tables(length):
    index = np.arange(length)
    fourier = np.exp(-2j * np.pi * (index[:, None] * index[None, :] % length) / length)
    frequency = np.where(index < length // 2, index, index - length).astype(np.float64)
    phase = np.exp(-1j * np.pi * frequency**2 / (4 * length))
    fresnel = (np.conj(fourier) * phase[None, :]) @ fourier / length
    odd = 2 * index + 1
    turn = odd[:, None] * odd[None, :] % (4 * length)
    shifted = np.exp(-2j * np.pi * turn / (4 * length)) / np.sqrt(length)
    left, right = [], []
    for matrix in (fresnel, shifted):
        for block in folded(matrix):
            high, low = split_table(left_form(block))
            left.append(np.concatenate([high, high, low], axis=1))
            high, low = split_table(left_form(np.conj(block)))
            left.append(np.concatenate([high, high, low], axis=1))
            high, low = split_table(left_form(np.conj(block)))
            right.append(np.concatenate([high, high, low], axis=0))
            high, low = split_table(left_form(block))
            right.append(np.concatenate([high, high, low], axis=0))
    order = np.concatenate([index[: length // 2], index[length // 2 :][::-1]])
    ramp = np.exp(1j * np.pi * order / length)
    tilt = ramp[:, None] * ramp[None, :]
    return np.stack(left), np.stack(right), np.stack([tilt.real, tilt.imag]).astype(np.float32)


def reversal(size):
    row = lax.broadcasted_iota(jnp.int32, (size, size), 0)
    col = lax.broadcasted_iota(jnp.int32, (size, size), 1)
    return jnp.where(row + col == size - 1, 1.0, 0.0).astype(F32)


def exact_dot(a, b):
    return jnp.dot(a, b, precision=lax.Precision.HIGHEST, preferred_element_type=F32)


def mirror_halves(x, flip):
    half = x.shape[0] // 2
    x = jnp.concatenate([x[:, :half], exact_dot(x[:, half:], flip)], axis=1)
    return jnp.concatenate([x[:half], exact_dot(flip, x[half:])], axis=0)


def prep_kernel(ids, probe, amplitudes, probe_out, amp_out):
    flip = reversal(probe.shape[-1] // 2)
    for part in range(2):
        probe_out[part] = mirror_halves(probe[part], flip)
    amp_out[...] = mirror_halves(amplitudes[ids[0]], flip)


def crop_kernel(peers, plane, waits, ids, positions, strips, rim, *rest):
    rest = rest[waits:]
    own_out, near_out = rest[:2]
    far_outs, rest = rest[2 : peers // 2 + 1], rest[peers // 2 + 1 :]
    outs = [own_out, near_out] + [far.at[i] for far in far_outs for i in range(2)]
    ext, cut, loaded, stored = rest
    rows, cols = rim.shape
    blocks = cols // LANES
    size = own_out.shape[-1]
    loads = []
    for block in range(blocks):
        columns = pl.ds(block * LANES, LANES)
        loads.append(
            pltpu.make_async_copy(
                strips.at[plane[0], plane[1], :, columns], ext.at[block, pl.ds(0, rows)], loaded.at[2 * block]
            )
        )
        loads.append(
            pltpu.make_async_copy(
                rim.at[:, columns], ext.at[block, pl.ds(rows, rows)], loaded.at[2 * block + 1]
            )
        )
    for copy in loads:
        copy.start()
    flip = reversal(size // 2)
    lane = lax.broadcasted_iota(jnp.int32, (size, LANES), 1)
    ext[blocks] = jnp.zeros((2 * rows, LANES), F32)
    for copy in loads:
        copy.wait()
    stores = []
    for offset in sorted(range(peers), key=lambda m: -(m // 2)):
        window = ids[0] ^ offset
        row_first = positions[window, 0] - ids[1] * rows
        col_first = positions[window, 1]
        block_first = col_first >> 7
        within = col_first & (LANES - 1)
        moved = [
            pltpu.roll(ext[block_first + i, pl.ds(row_first, size), :], (LANES - within) & (LANES - 1), 1)
            for i in range(size // LANES + 1)
        ]
        keep = lane < LANES - within
        picked = [jnp.where(keep, moved[i], moved[i + 1]) for i in range(size // LANES)]
        cut[offset] = mirror_halves(jnp.concatenate(picked, axis=1), flip)
        copy = pltpu.make_async_copy(cut.at[offset], outs[offset], stored.at[offset])
        copy.start()
        stores.append(copy)
    for copy in stores:
        copy.wait()


def place_kernel(peers, waits, ids, positions, *rest):
    own_in, near_in = rest[:2]
    far_ins, rest = rest[2:peers], rest[peers + waits :]
    pieces = [own_in, near_in]
    for i in range(0, len(far_ins), 2):
        pieces += [far_ins[i].at[0], far_ins[i + 1]]
    own, rim, ext, got, loaded, stored = rest
    rows, cols = own.shape
    blocks = cols // LANES
    size = own_in.shape[-1]
    loads = [
        pltpu.make_async_copy(pieces[offset], got.at[offset], loaded.at[offset]) for offset in range(peers)
    ]
    for copy in loads:
        copy.start()
    flip = reversal(size // 2)
    lane = lax.broadcasted_iota(jnp.int32, (size, LANES), 1)
    ext[...] = jnp.zeros(ext.shape, F32)
    for offset in range(peers):
        window = ids[0] ^ offset
        row_first = positions[window, 0] - ids[1] * rows
        col_first = positions[window, 1]
        block_first = col_first >> 7
        within = col_first & (LANES - 1)
        loads[offset].wait()
        plain = mirror_halves(got[offset], flip)
        moved = [pltpu.roll(plain[:, i * LANES : (i + 1) * LANES], within, 1) for i in range(size // LANES)]
        keep = lane >= within
        zero = jnp.zeros((size, LANES), F32)
        moved = [zero] + moved + [zero]
        for i in range(size // LANES + 1):
            place = (block_first + i, pl.ds(row_first, size))
            ext[place] = ext[place] + jnp.where(keep, moved[i + 1], moved[i])
    stores = []
    for block in range(blocks):
        columns = pl.ds(block * LANES, LANES)
        stores.append(
            pltpu.make_async_copy(ext.at[block, pl.ds(rows, rows)], rim.at[:, columns], stored.at[2 * block])
        )
        stores.append(
            pltpu.make_async_copy(ext.at[block, pl.ds(0, rows)], own.at[:, columns], stored.at[2 * block + 1])
        )
    for copy in stores:
        copy.start()
    for copy in stores:
        copy.wait()


def split_value(x):
    high = x.astype(BF16)
    low = (x - high.astype(F32)).astype(BF16)
    return high, low


def sandwich(re, im, left, right, base, conj):
    half = re.shape[0] // 2

    def fold(x):
        upper, lower = x[:half], x[half:]
        even, odd = upper + lower, upper - lower
        parts = []
        for y in (even, odd):
            near, far = y[:, :half], y[:, half:]
            parts.append((near + far, near - far))
        return parts

    re_parts, im_parts = fold(re), fold(im)
    middle = []
    for b in range(2):
        field = jnp.concatenate(
            [jnp.concatenate([re_parts[a][b], im_parts[a][b]], axis=1) for a in range(2)], axis=0
        )
        high, low = split_value(field)
        middle.append(
            jnp.dot(
                jnp.concatenate([high, low, high], axis=1),
                right[base + 2 * b + conj],
                preferred_element_type=F32,
            )
        )
    done = []
    for a in range(2):
        rows = slice(a * half, (a + 1) * half)
        field = jnp.concatenate(
            [
                jnp.concatenate([middle[b][rows, :half] for b in range(2)], axis=1),
                jnp.concatenate([middle[b][rows, half:] for b in range(2)], axis=1),
            ],
            axis=0,
        )
        high, low = split_value(field)
        done.append(
            jnp.dot(
                left[base + 2 * a + conj],
                jnp.concatenate([high, low, high], axis=0),
                preferred_element_type=F32,
            )
        )

    def unfold(even, odd):
        rows = jnp.concatenate([even + odd, even - odd], axis=0)
        near, far = rows[:, :half], rows[:, half:]
        return jnp.concatenate([near + far, near - far], axis=1)

    return (
        unfold(done[0][:half], done[1][:half]),
        unfold(done[0][half:], done[1][half:]),
    )


def optics_kernel(peers, per_device, ids, probe, amplitude, left, right, tilt, *rest):
    chunks = 2 * per_device
    groups = peers // 2 + 1
    crops, pieces = [], []
    for chunk in range(chunks):
        got = rest[chunk * peers : (chunk + 1) * peers]
        crops += list(got[:2])
        for i in range(2, peers, 2):
            crops += [got[i].at[0], got[i + 1]]
    rest = rest[chunks * peers :]
    for chunk in range(chunks):
        out = rest[chunk * groups : (chunk + 1) * groups]
        pieces += list(out[:2])
        for far in out[2:]:
            pieces += [far.at[0], far.at[1]]
    kept, handed = rest[chunks * groups : chunks * groups + 2]
    rest = rest[chunks * groups + 2 :]
    trans, history, terms, grad, loaded, stored = rest
    layers = peers * per_device
    me = ids[0]
    for j in range(per_device):
        for offset in range(peers):
            at = (me ^ offset) * per_device + j
            for part in range(2):
                pltpu.make_async_copy(
                    crops[(j * 2 + part) * peers + offset], trans.at[at, part], loaded.at[2 * at + part]
                ).start()
    history[0] = probe[...]

    def mixed(layer):
        for part in range(2):
            pltpu.make_async_copy(crops[0], trans.at[layer, part], loaded.at[2 * layer + part]).wait()
        t_re, t_im = trans[layer, 0], trans[layer, 1]
        w_re, w_im = history[layer, 0], history[layer, 1]
        return t_re * w_re - t_im * w_im, t_re * w_im + t_im * w_re

    def forward(layer, carry):
        re, im = mixed(layer)
        re, im = sandwich(re, im, left, right, 0, 0)
        history[layer + 1, 0] = re
        history[layer + 1, 1] = im
        return carry

    lax.fori_loop(0, layers - 1, forward, 0)
    re, im = mixed(layers - 1)
    d_re, d_im = tilt[0], tilt[1]
    re, im = re * d_re - im * d_im, re * d_im + im * d_re
    re, im = sandwich(re, im, left, right, 4, 0)
    factor = 1.0 - amplitude[...] / jnp.sqrt(re * re + im * im + 1.0)
    re, im = sandwich(re * factor, im * factor, left, right, 4, 1)
    back_re, back_im = re * d_re + im * d_im, im * d_re - re * d_im

    def collect(layer, back_re, back_im):
        w_re, w_im = history[layer, 0], history[layer, 1]
        terms[layer, 0] = w_re * back_re + w_im * back_im
        terms[layer, 1] = w_re * back_im - w_im * back_re
        owner, j_now = lax.div(layer, per_device), lax.rem(layer, per_device)
        for j in range(per_device):
            for offset in range(peers):

                @pl.when((owner == me ^ offset) & (j_now == j))
                def _():
                    for part in range(2):
                        pltpu.make_async_copy(
                            terms.at[layer, part],
                            pieces[(j * 2 + part) * peers + offset],
                            stored.at[2 * layer + part],
                        ).start()

        t_re, t_im = trans[layer, 0], trans[layer, 1]
        grad[0] = t_re * back_re + t_im * back_im
        grad[1] = t_re * back_im - t_im * back_re

    collect(layers - 1, back_re, back_im)

    def backward(step, carry):
        back_re, back_im = sandwich(grad[0], grad[1], left, right, 0, 1)
        collect(layers - 2 - step, back_re, back_im)
        return carry

    lax.fori_loop(0, layers - 1, backward, 0)
    flip = reversal(grad.shape[-1] // 2)
    share_rows = kept.shape[2]
    for part in range(2):
        grad[part] = mirror_halves(grad[part], flip)
    for offset in range(peers):
        first = pl.multiple_of((me ^ offset) * share_rows, share_rows)
        target = handed if offset % 2 else kept
        target[offset // 2] = grad[:, pl.ds(first, share_rows), :]
    for layer in range(layers):
        for part in range(2):
            pltpu.make_async_copy(terms.at[layer, part], pieces[0], stored.at[2 * layer + part]).wait()


SMEM_SPEC = pl.BlockSpec(memory_space=pltpu.SMEM)
VMEM_SPEC = pl.BlockSpec(memory_space=pltpu.VMEM)
HBM_SPEC = pl.BlockSpec(memory_space=pltpu.HBM)


def gate_kernel(*refs):
    pass


def gate(passed, waits):
    total = len(passed)
    if not total or not waits:
        return passed
    return run_kernel(
        gate_kernel,
        "gate",
        tuple(shape(*x.shape) for x in passed),
        [HBM_SPEC] * (total + len(waits)),
        (HBM_SPEC,) * total,
        [],
        0.1,
        aliases={i: i for i in range(total)},
    )(*passed, *waits)


def run_kernel(kernel, name, out_shapes, in_specs, out_specs, scratch, micros, mebibytes=16, aliases={}):
    return pl.pallas_call(
        kernel,
        name=name,
        out_shape=out_shapes,
        in_specs=in_specs,
        out_specs=out_specs,
        scratch_shapes=scratch,
        input_output_aliases=aliases,
        compiler_params=pltpu.CompilerParams(vmem_limit_bytes=mebibytes * 2**20),
        cost_estimate=pl.CostEstimate(
            flops=int(micros * 1e6), bytes_accessed=int(micros * 1e3), transcendentals=0
        ),
    )


def shape(*dims):
    return jax.ShapeDtypeStruct(dims, F32)


def swap(x, axis, offset):
    peers = lax.axis_size(axis)
    return lax.ppermute(x, axis, [(i, i ^ offset) for i in range(peers)])


def exchanged(mine, waits=()):
    got = [mine[0], swap(mine[1], "depth", 1)]
    for i, pair in enumerate(mine[2:]):
        across = swap(pair, "depth", 2 * (i + 1))
        (across,) = gate([across], waits)
        got += [across, swap(across[1], "depth", 1)]
    return got


def echo(x):
    return swap(x[:8, :LANES], "depth", 1)


def shift(x, axis, by):
    peers = lax.axis_size(axis)
    return lax.ppermute(x, axis, [(i, i + by) for i in range(peers) if 0 <= i + by < peers])


def body(transmission, probe_field, scan_positions, amplitudes):
    size = probe_field.shape[-1]
    per_device, _, rows, cols = transmission.shape
    peers = lax.axis_size("depth")
    tiles = lax.axis_size("tile")
    ids = jnp.stack([lax.axis_index("depth"), lax.axis_index("tile")]).astype(jnp.int32)
    left, right, tilt = (jnp.asarray(x) for x in optics_tables(size))

    probe, amplitude = run_kernel(
        prep_kernel,
        "prep",
        (shape(2, size, size), shape(size, size)),
        [SMEM_SPEC, VMEM_SPEC, VMEM_SPEC],
        [VMEM_SPEC, VMEM_SPEC],
        [],
        2,
    )(ids, probe_field, amplitudes)

    chunks = [(j, part) for j in range(per_device) for part in range(2)]
    ahead = 2
    strips = [transmission[c[0], c[1]] for c in chunks]
    group = (shape(size, size),) * 2 + (shape(2, size, size),) * (peers // 2 - 1)
    groups = len(group)
    crops = []
    for k, c in enumerate(chunks):
        rim = shift(strips[k], "tile", -1)
        waits = crops[k - ahead][2::2] if k >= ahead else [probe, amplitude]
        mine = run_kernel(
            functools.partial(crop_kernel, peers, c, len(waits)),
            "crop",
            group,
            [SMEM_SPEC, SMEM_SPEC] + [HBM_SPEC] * (2 + len(waits)),
            (HBM_SPEC,) * groups,
            [
                pltpu.VMEM((cols // LANES + 1, 2 * rows, LANES), F32),
                pltpu.VMEM((peers, size, size), F32),
                pltpu.SemaphoreType.DMA((2 * cols // LANES,)),
                pltpu.SemaphoreType.DMA((peers,)),
            ],
            2,
        )(ids, scan_positions, transmission, rim, *waits)
        strips[k + ahead : k + ahead + 1] = gate(strips[k + ahead : k + ahead + 1], mine[:1])
        crops.append(exchanged(mine))
    layers = per_device * peers
    result = run_kernel(
        functools.partial(optics_kernel, peers, per_device),
        "optics",
        group * len(chunks) + (shape(peers // 2, 2, size // peers, size),) * 2,
        [SMEM_SPEC] + [VMEM_SPEC] * 5 + [HBM_SPEC] * (len(chunks) * peers),
        (HBM_SPEC,) * (len(chunks) * groups) + (VMEM_SPEC,) * 2,
        [
            pltpu.VMEM((layers, 2, size, size), F32),
            pltpu.VMEM((layers, 2, size, size), F32),
            pltpu.VMEM((layers, 2, size, size), F32),
            pltpu.VMEM((2, size, size), F32),
            pltpu.SemaphoreType.DMA((2 * layers,)),
            pltpu.SemaphoreType.DMA((2 * layers,)),
        ],
        15,
        32,
    )(ids, probe, amplitude, left, right, tilt, *[x for got in crops for x in got])

    kept, handed = result[-2:]
    probe_halves = kept + swap(handed, "depth", 1)
    probe_grad = probe_halves
    step = 2
    while step < peers:
        probe_grad = probe_grad[:1] + swap(probe_grad[1:], "depth", step)
        step *= 2
    probe_steps = [probe_grad[0]]
    step = 1
    while step < tiles:
        probe_steps.append(probe_steps[-1] + swap(probe_steps[-1], "tile", step))
        step *= 2

    own, rim_back, returned = {}, {}, []
    order = list(reversed(chunks))
    for k, c in enumerate(order):
        at = chunks.index(c) * groups
        mine = result[at : at + groups]
        if k == 0:
            mine = gate(mine, probe_steps[:1])
        if k >= ahead:
            mine = gate(mine, returned[k - ahead][2::2] + [own[order[k - ahead]]])
        returned.append(exchanged(mine, [own[order[k - 1]]] if k else []))
        waits = [] if k else probe_steps[-1:]
        own[c], outside = run_kernel(
            functools.partial(place_kernel, peers, len(waits)),
            "place",
            (shape(rows, cols), shape(rows, cols)),
            [SMEM_SPEC, SMEM_SPEC] + [HBM_SPEC] * (peers + len(waits)),
            (HBM_SPEC, HBM_SPEC),
            [
                pltpu.VMEM((cols // LANES + 1, 2 * rows, LANES), F32),
                pltpu.VMEM((peers, size, size), F32),
                pltpu.SemaphoreType.DMA((peers,)),
                pltpu.SemaphoreType.DMA((2 * cols // LANES,)),
            ],
            2,
        )(ids, scan_positions, *returned[k], *waits)
        if k >= ahead:
            (outside,) = gate([outside], [echo(rim_back[order[k - ahead]])])
        rim_back[c] = shift(outside, "tile", 1)

    rim_back[order[-2]] = gate([rim_back[order[-2]]], [echo(rim_back[order[-2]])])[0]
    object_grad = jnp.stack(
        [
            jnp.stack([own[(j, part)] + rim_back[(j, part)] for part in range(2)])
            for j in range(per_device)
        ]
    )
    return (object_grad, probe_steps[-1])


def solution(mesh):
    placed = (P("depth", None, "tile", None), P(), P("tile", None), P("tile", None, None))
    return jax.shard_map(
        body,
        mesh=mesh,
        in_specs=placed,
        out_specs=(P("depth", None, "tile", None), P(None, "depth", None)),
        check_vma=False,
    )
```

```python
import functools

import jax
import jax.numpy as jnp
import ml_dtypes
import numpy as np
from jax import lax
from jax.experimental import pallas as pl
from jax.experimental.pallas import tpu as pltpu
from jax.sharding import PartitionSpec as P

LANES = 128
F32 = jnp.float32
BF16 = jnp.bfloat16


def split_table(table):
    high = table.astype(np.float32).astype(ml_dtypes.bfloat16)
    low = (table - high.astype(np.float64)).astype(np.float32).astype(ml_dtypes.bfloat16)
    return high, low


def left_form(matrix):
    return np.block([[matrix.real, -matrix.imag], [matrix.imag, matrix.real]])


def folded(matrix):
    half = matrix.shape[0] // 2
    near = matrix[:half, :half]
    mirrored = matrix[:half, half:][:, ::-1]
    return (near + mirrored) / 2, (near - mirrored) / 2


def optics_tables(length):
    index = np.arange(length)
    fourier = np.exp(-2j * np.pi * (index[:, None] * index[None, :] % length) / length)
    frequency = np.where(index < length // 2, index, index - length).astype(np.float64)
    phase = np.exp(-1j * np.pi * frequency**2 / (4 * length))
    fresnel = (np.conj(fourier) * phase[None, :]) @ fourier / length
    odd = 2 * index + 1
    turn = odd[:, None] * odd[None, :] % (4 * length)
    shifted = np.exp(-2j * np.pi * turn / (4 * length)) / np.sqrt(length)
    tables = []
    for matrix in (fresnel, shifted):
        for block in folded(matrix):
            for form in (left_form(block), left_form(np.conj(block))):
                tables.append(np.stack(split_table(form)))
    order = np.concatenate([index[: length // 2], index[length // 2 :][::-1]])
    ramp = np.exp(1j * np.pi * order / length)
    tilt = ramp[:, None] * ramp[None, :]
    return np.stack(tables), np.stack([tilt.real, tilt.imag]).astype(np.float32)


def reversal(size):
    row = lax.broadcasted_iota(jnp.int32, (size, size), 0)
    col = lax.broadcasted_iota(jnp.int32, (size, size), 1)
    return jnp.where(row + col == size - 1, 1.0, 0.0).astype(BF16)


def exact_dot(a, b):
    moving, table = (a, b) if b.dtype == BF16 else (b, a)
    total = None
    for part in range(3):
        piece = moving.astype(BF16)
        moving = moving - piece.astype(F32)
        done = jnp.dot(*((piece, b) if b.dtype == BF16 else (a, piece)), preferred_element_type=F32)
        total = done if total is None else total + done
    return total


def mirror_halves(fields, flip):
    count, size = len(fields), fields[0].shape[0]
    half = size // 2
    right = exact_dot(jnp.concatenate([x[:, half:] for x in fields], axis=0), flip)
    fields = [
        jnp.concatenate([x[:, :half], right[i * size : (i + 1) * size]], axis=1) for i, x in enumerate(fields)
    ]
    lower = exact_dot(flip, jnp.concatenate([x[half:] for x in fields], axis=1))
    return [
        jnp.concatenate([x[:half], lower[:, i * size : (i + 1) * size]], axis=0) for i, x in enumerate(fields)
    ]


def prep_kernel(ids, probe, amplitudes, probe_out, amp_out):
    flip = reversal(probe.shape[-1] // 2)
    probe_out[0], probe_out[1], amp_out[...] = mirror_halves([probe[0], probe[1], amplitudes[ids[0]]], flip)


def crop_kernel(peers, plane, waits, ids, positions, strips, rim, *rest):
    rest = rest[waits:]
    own_out, near_out = rest[:2]
    far_outs, rest = rest[2 : peers // 2 + 1], rest[peers // 2 + 1 :]
    outs = [own_out, near_out] + [far.at[i] for far in far_outs for i in range(2)]
    ext, cut, loaded, stored = rest
    rows, cols = rim.shape
    blocks = cols // LANES
    size = own_out.shape[-1]
    loads = []
    for block in range(blocks):
        columns = pl.ds(block * LANES, LANES)
        loads.append(
            pltpu.make_async_copy(
                strips.at[plane[0], plane[1], :, columns], ext.at[block, pl.ds(0, rows)], loaded.at[2 * block]
            )
        )
        loads.append(
            pltpu.make_async_copy(
                rim.at[:, columns], ext.at[block, pl.ds(rows, rows)], loaded.at[2 * block + 1]
            )
        )
    for copy in loads:
        copy.start()
    flip = reversal(size // 2)
    lane = lax.broadcasted_iota(jnp.int32, (size, LANES), 1)
    ext[blocks] = jnp.zeros((2 * rows, LANES), F32)
    for copy in loads:
        copy.wait()
    stores = []
    for pair in sorted(range(0, peers, 2), reverse=True):
        fields = []
        for offset in (pair, pair + 1):
            window = ids[0] ^ offset
            row_first = positions[window, 0] - ids[1] * rows
            col_first = positions[window, 1]
            block_first = col_first >> 7
            within = col_first & (LANES - 1)
            moved = [
                pltpu.roll(
                    ext[block_first + i, pl.ds(row_first, size), :], (LANES - within) & (LANES - 1), 1
                )
                for i in range(size // LANES + 1)
            ]
            keep = lane < LANES - within
            picked = [jnp.where(keep, moved[i], moved[i + 1]) for i in range(size // LANES)]
            fields.append(jnp.concatenate(picked, axis=1))
        fields = mirror_halves(fields, flip)
        for i, offset in enumerate((pair, pair + 1)):
            cut[offset] = fields[i]
            copy = pltpu.make_async_copy(cut.at[offset], outs[offset], stored.at[offset])
            copy.start()
            stores.append(copy)
    for copy in stores:
        copy.wait()


def place_kernel(peers, ids, positions, *rest):
    own_in, near_in = rest[:2]
    far_ins = rest[2:peers]
    pieces = [own_in, near_in]
    for i in range(0, len(far_ins), 2):
        pieces += [far_ins[i].at[0], far_ins[i + 1]]
    own, rim, ext, got, loaded, stored = rest[peers:]
    rows, cols = own.shape
    blocks = cols // LANES
    size = own_in.shape[-1]
    loads = [
        pltpu.make_async_copy(pieces[offset], got.at[offset], loaded.at[offset]) for offset in range(peers)
    ]
    for copy in loads:
        copy.start()
    flip = reversal(size // 2)
    lane = lax.broadcasted_iota(jnp.int32, (size, LANES), 1)
    ext[...] = jnp.zeros(ext.shape, F32)
    for copy in loads:
        copy.wait()
    fields = mirror_halves([got[offset] for offset in range(peers)], flip)
    for offset in range(peers):
        window = ids[0] ^ offset
        row_first = positions[window, 0] - ids[1] * rows
        col_first = positions[window, 1]
        block_first = col_first >> 7
        within = col_first & (LANES - 1)
        moved = [
            pltpu.roll(fields[offset][:, i * LANES : (i + 1) * LANES], within, 1) for i in range(size // LANES)
        ]
        keep = lane >= within
        zero = jnp.zeros((size, LANES), F32)
        moved = [zero] + moved + [zero]
        for i in range(size // LANES + 1):
            place = (block_first + i, pl.ds(row_first, size))
            ext[place] = ext[place] + jnp.where(keep, moved[i + 1], moved[i])
    stores = []
    for block in range(blocks):
        columns = pl.ds(block * LANES, LANES)
        stores.append(
            pltpu.make_async_copy(ext.at[block, pl.ds(rows, rows)], rim.at[:, columns], stored.at[2 * block])
        )
        stores.append(
            pltpu.make_async_copy(ext.at[block, pl.ds(0, rows)], own.at[:, columns], stored.at[2 * block + 1])
        )
    for copy in stores:
        copy.start()
    for copy in stores:
        copy.wait()


def split_value(x):
    high = x.astype(BF16)
    low = (x - high.astype(F32)).astype(BF16)
    return high, low


def dot32(a, b):
    return jnp.dot(a, b, preferred_element_type=F32)


def sandwich(re, im, tables, base, conj):
    half = re.shape[0] // 2

    def fold(x):
        upper, lower = x[:half], x[half:]
        even, odd = upper + lower, upper - lower
        parts = []
        for y in (even, odd):
            near, far = y[:, :half], y[:, half:]
            parts.append((near + far, near - far))
        return parts

    re_parts, im_parts = fold(re), fold(im)
    middle = []
    for b in range(2):
        field = jnp.concatenate(
            [jnp.concatenate([re_parts[a][b], im_parts[a][b]], axis=1) for a in range(2)], axis=0
        )
        high, low = split_value(field)
        middle.append(
            dot32(high, tables[base + 2 * b + 1 - conj, 0])
            + dot32(low, tables[base + 2 * b + 1 - conj, 0])
            + dot32(high, tables[base + 2 * b + 1 - conj, 1])
        )
    done = []
    for a in range(2):
        rows = slice(a * half, (a + 1) * half)
        field = jnp.concatenate(
            [
                jnp.concatenate([middle[b][rows, :half] for b in range(2)], axis=1),
                jnp.concatenate([middle[b][rows, half:] for b in range(2)], axis=1),
            ],
            axis=0,
        )
        high, low = split_value(field)
        done.append(
            dot32(tables[base + 2 * a + conj, 0], high)
            + dot32(tables[base + 2 * a + conj, 0], low)
            + dot32(tables[base + 2 * a + conj, 1], high)
        )

    def unfold(even, odd):
        rows = jnp.concatenate([even + odd, even - odd], axis=0)
        near, far = rows[:, :half], rows[:, half:]
        return jnp.concatenate([near + far, near - far], axis=1)

    return (
        unfold(done[0][:half], done[1][:half]),
        unfold(done[0][half:], done[1][half:]),
    )


def optics_kernel(peers, per_device, ids, probe_in, amplitude_in, tables_in, tilt_in, *rest):
    chunks = 2 * per_device
    groups = peers // 2 + 1
    crops, pieces = [], []
    for chunk in range(chunks):
        got = rest[chunk * peers : (chunk + 1) * peers]
        crops += list(got[:2])
        for i in range(2, peers, 2):
            crops += [got[i].at[0], got[i + 1]]
    rest = rest[chunks * peers :]
    for chunk in range(chunks):
        out = rest[chunk * groups : (chunk + 1) * groups]
        pieces += list(out[:2])
        for far in out[2:]:
            pieces += [far.at[0], far.at[1]]
    kept, handed = rest[chunks * groups : chunks * groups + 2]
    rest = rest[chunks * groups + 2 :]
    trans, history, terms, grad, tables, tilt, amplitude, fixed, loaded, stored = rest
    size = grad.shape[-1]
    share = size // peers
    layers = peers * per_device
    me = ids[0]
    half = tables.shape[0] // 2
    settings = [
        pltpu.make_async_copy(probe_in, history.at[0], fixed.at[0]),
        pltpu.make_async_copy(tables_in.at[pl.ds(0, half)], tables.at[pl.ds(0, half)], fixed.at[1]),
        pltpu.make_async_copy(tables_in.at[pl.ds(half, half)], tables.at[pl.ds(half, half)], fixed.at[2]),
        pltpu.make_async_copy(tilt_in, tilt, fixed.at[3]),
        pltpu.make_async_copy(amplitude_in, amplitude, fixed.at[4]),
    ]
    for copy in settings[:2]:
        copy.start()
    for j in range(per_device):
        for offset in range(peers):
            at = (me ^ offset) * per_device + j
            for part in range(2):
                pltpu.make_async_copy(
                    crops[(j * 2 + part) * peers + offset], trans.at[at, part], loaded.at[2 * at + part]
                ).start()
    for copy in settings[2:]:
        copy.start()
    for copy in settings[:2]:
        copy.wait()

    def mixed(layer):
        for part in range(2):
            pltpu.make_async_copy(crops[0], trans.at[layer, part], loaded.at[2 * layer + part]).wait()
        t_re, t_im = trans[layer, 0], trans[layer, 1]
        w_re, w_im = history[layer, 0], history[layer, 1]
        return t_re * w_re - t_im * w_im, t_re * w_im + t_im * w_re

    def forward(layer, carry):
        re, im = mixed(layer)
        re, im = sandwich(re, im, tables, 0, 0)
        history[layer + 1, 0] = re
        history[layer + 1, 1] = im
        return carry

    lax.fori_loop(0, layers - 1, forward, 0)
    re, im = mixed(layers - 1)
    for copy in settings[2:]:
        copy.wait()
    d_re, d_im = tilt[0], tilt[1]
    re, im = re * d_re - im * d_im, re * d_im + im * d_re
    re, im = sandwich(re, im, tables, 4, 0)
    factor = 1.0 - amplitude[...] / jnp.sqrt(re * re + im * im + 1.0)
    re, im = sandwich(re * factor, im * factor, tables, 4, 1)
    back_re, back_im = re * d_re + im * d_im, im * d_re - re * d_im

    def collect(layer, back_re, back_im):
        w_re, w_im = history[layer, 0], history[layer, 1]
        terms[layer, 0] = w_re * back_re + w_im * back_im
        terms[layer, 1] = w_re * back_im - w_im * back_re
        owner, j_now = lax.div(layer, per_device), lax.rem(layer, per_device)
        for j in range(per_device):
            for offset in range(peers):

                @pl.when((owner == me ^ offset) & (j_now == j))
                def _():
                    for part in range(2):
                        pltpu.make_async_copy(
                            terms.at[layer, part],
                            pieces[(j * 2 + part) * peers + offset].at[pl.ds(0, size)],
                            stored.at[2 * layer + part],
                        ).start()

        t_re, t_im = trans[layer, 0], trans[layer, 1]
        grad[0] = t_re * back_re + t_im * back_im
        grad[1] = t_re * back_im - t_im * back_re

    collect(layers - 1, back_re, back_im)

    def backward(step, carry):
        back_re, back_im = sandwich(grad[0], grad[1], tables, 0, 1)
        collect(layers - 2 - step, back_re, back_im)
        return carry

    lax.fori_loop(0, layers - 1, backward, 0)
    grad[0], grad[1] = mirror_halves([grad[0], grad[1]], reversal(size // 2))
    shares = []
    for offset in range(peers):
        first = pl.multiple_of((me ^ offset) * share, share)
        for part in range(2):
            shares.append(
                pltpu.make_async_copy(
                    grad.at[part, pl.ds(first, share)],
                    (kept, handed)[offset % 2].at[offset // 2, part],
                    fixed.at[2 * offset + part],
                )
            )
    for copy in shares:
        copy.start()
    for layer in range(layers):
        for part in range(2):
            pltpu.make_async_copy(
                terms.at[layer, part], pieces[0].at[pl.ds(0, size)], stored.at[2 * layer + part]
            ).wait()
    for copy in shares:
        copy.wait()


SMEM_SPEC = pl.BlockSpec(memory_space=pltpu.SMEM)
VMEM_SPEC = pl.BlockSpec(memory_space=pltpu.VMEM)
HBM_SPEC = pl.BlockSpec(memory_space=pltpu.HBM)


def gate_kernel(*refs):
    pass


def gate(passed, waits):
    total = len(passed)
    if not total or not waits:
        return passed
    return run_kernel(
        gate_kernel,
        "gate",
        tuple(shape(*x.shape) for x in passed),
        [HBM_SPEC] * (total + len(waits)),
        (HBM_SPEC,) * total,
        [],
        0.1,
        aliases={i: i for i in range(total)},
    )(*passed, *waits)


def run_kernel(kernel, name, out_shapes, in_specs, out_specs, scratch, micros, mebibytes=16, aliases={}):
    return pl.pallas_call(
        kernel,
        name=name,
        out_shape=out_shapes,
        in_specs=in_specs,
        out_specs=out_specs,
        scratch_shapes=scratch,
        input_output_aliases=aliases,
        compiler_params=pltpu.CompilerParams(vmem_limit_bytes=mebibytes * 2**20),
        cost_estimate=pl.CostEstimate(
            flops=int(micros * 1e6), bytes_accessed=int(micros * 1e3), transcendentals=0
        ),
    )


def shape(*dims):
    return jax.ShapeDtypeStruct(dims, F32)


def swap(x, axis, offset):
    peers = lax.axis_size(axis)
    return lax.ppermute(x, axis, [(i, i ^ offset) for i in range(peers)])


def exchanged(mine, waits=()):
    got = [mine[0], swap(mine[1], "depth", 1)]
    for i, pair in enumerate(mine[2:]):
        across = swap(pair, "depth", 2 * (i + 1))
        (across,) = gate([across], waits)
        got += [across, swap(across[1], "depth", 1)]
    return got


def echo(x):
    return swap(x[:8, :LANES], "depth", 1)


def shift(x, axis, by):
    peers = lax.axis_size(axis)
    return lax.ppermute(x, axis, [(i, i + by) for i in range(peers) if 0 <= i + by < peers])


def body(transmission, probe_field, scan_positions, amplitudes):
    size = probe_field.shape[-1]
    per_device, _, rows, cols = transmission.shape
    peers = lax.axis_size("depth")
    tiles = lax.axis_size("tile")
    ids = jnp.stack([lax.axis_index("depth"), lax.axis_index("tile")]).astype(jnp.int32)
    tables, tilt = (jnp.asarray(x) for x in optics_tables(size))

    probe, amplitude = run_kernel(
        prep_kernel,
        "prep",
        (shape(2, size, size), shape(size, size)),
        [SMEM_SPEC, VMEM_SPEC, VMEM_SPEC],
        [VMEM_SPEC, VMEM_SPEC],
        [],
        2,
    )(ids, probe_field, amplitudes)

    chunks = [(j, part) for j in range(per_device) for part in range(2)]
    ahead = 2
    strips = [transmission[c[0], c[1]] for c in chunks]
    group = (shape(size, size),) * 2 + (shape(2, size, size),) * (peers // 2 - 1)
    groups = len(group)
    crops = []
    for k, c in enumerate(chunks):
        rim = shift(strips[k], "tile", -1)
        waits = crops[k - ahead][2::2] if k >= ahead else [probe, amplitude]
        mine = run_kernel(
            functools.partial(crop_kernel, peers, c, len(waits)),
            "crop",
            group,
            [SMEM_SPEC, SMEM_SPEC] + [HBM_SPEC] * (2 + len(waits)),
            (HBM_SPEC,) * groups,
            [
                pltpu.VMEM((cols // LANES + 1, 2 * rows, LANES), F32),
                pltpu.VMEM((peers, size, size), F32),
                pltpu.SemaphoreType.DMA((2 * cols // LANES,)),
                pltpu.SemaphoreType.DMA((peers,)),
            ],
            2,
        )(ids, scan_positions, transmission, rim, *waits)
        strips[k + ahead : k + ahead + 1] = gate(strips[k + ahead : k + ahead + 1], mine[:1])
        crops.append(exchanged(mine))
    layers = per_device * peers
    result = run_kernel(
        functools.partial(optics_kernel, peers, per_device),
        "optics",
        group * len(chunks) + (shape(peers // 2, 2, size // peers, size),) * 2,
        [SMEM_SPEC] + [HBM_SPEC] * (4 + len(chunks) * peers),
        (HBM_SPEC,) * (len(chunks) * groups + 2),
        [
            pltpu.VMEM((layers, 2, size, size), F32),
            pltpu.VMEM((layers, 2, size, size), F32),
            pltpu.VMEM((layers, 2, size, size), F32),
            pltpu.VMEM((2, size, size), F32),
            pltpu.VMEM(tables.shape, BF16),
            pltpu.VMEM(tilt.shape, F32),
            pltpu.VMEM((size, size), F32),
            pltpu.SemaphoreType.DMA((max(5, 2 * peers),)),
            pltpu.SemaphoreType.DMA((2 * layers,)),
            pltpu.SemaphoreType.DMA((2 * layers,)),
        ],
        15,
        32,
    )(ids, probe, amplitude, tables, tilt, *[x for got in crops for x in got])

    kept, handed = result[-2:]
    probe_halves = kept + swap(handed, "depth", 1)
    probe_grad = probe_halves
    step = 2
    while step < peers:
        probe_grad = probe_grad[:1] + swap(probe_grad[1:], "depth", step)
        step *= 2
    probe_steps = [probe_grad[0]]
    step = tiles // 2
    while step:
        probe_steps.append(probe_steps[-1] + swap(probe_steps[-1], "tile", step))
        step //= 2

    own, rim_back, returned = {}, {}, []
    order = list(reversed(chunks))
    for k, c in enumerate(order):
        at = chunks.index(c) * groups
        mine = result[at : at + groups]
        if k == 0:
            mine = gate(mine, [probe_steps[0]])
        if k >= ahead:
            mine = gate(mine, returned[k - ahead][2::2] + [own[order[k - ahead]]])
        before = [own[order[k - 1]]] if k else probe_steps[-2:-1]
        if k == 1:
            before.append(probe_steps[-1])
        returned.append(exchanged(mine, before))
        mine = run_kernel(
            functools.partial(place_kernel, peers),
            "place",
            (shape(rows, cols), shape(rows, cols)),
            [SMEM_SPEC, SMEM_SPEC] + [HBM_SPEC] * peers,
            (HBM_SPEC, HBM_SPEC),
            [
                pltpu.VMEM((cols // LANES + 1, 2 * rows, LANES), F32),
                pltpu.VMEM((peers, size, size), F32),
                pltpu.SemaphoreType.DMA((peers,)),
                pltpu.SemaphoreType.DMA((2 * cols // LANES,)),
            ],
            2,
        )(ids, scan_positions, *returned[k])
        own[c], outside = mine[:2]
        if k >= ahead:
            (outside,) = gate([outside], [echo(echo(rim_back[order[k - ahead]]))])
        rim_back[c] = shift(outside, "tile", 1)

    rim_back[order[-2]] = gate([rim_back[order[-2]]], [echo(rim_back[order[-2]])])[0]
    object_grad = jnp.stack(
        [
            jnp.stack([own[(j, part)] + rim_back[(j, part)] for part in range(2)])
            for j in range(per_device)
        ]
    )
    return (object_grad, probe_steps[-1])


def solution(mesh):
    placed = (P("depth", None, "tile", None), P(), P("tile", None), P("tile", None, None))
    return jax.shard_map(
        body,
        mesh=mesh,
        in_specs=placed,
        out_specs=(P("depth", None, "tile", None), P(None, "depth", None)),
        check_vma=False,
    )
```

```python
import functools

import jax
import jax.numpy as jnp
import ml_dtypes
import numpy as np
from jax import lax
from jax.experimental import pallas as pl
from jax.experimental.pallas import tpu as pltpu
from jax.sharding import PartitionSpec as P

LANES = 128
F32 = jnp.float32
BF16 = jnp.bfloat16


def split_table(table):
    high = table.astype(np.float32).astype(ml_dtypes.bfloat16)
    low = (table - high.astype(np.float64)).astype(np.float32).astype(ml_dtypes.bfloat16)
    return high, low


def left_form(matrix):
    return np.block([[matrix.real, -matrix.imag], [matrix.imag, matrix.real]])


def folded(matrix):
    half = matrix.shape[0] // 2
    near = matrix[:half, :half]
    mirrored = matrix[:half, half:][:, ::-1]
    return (near + mirrored) / 2, (near - mirrored) / 2


def optics_tables(length):
    index = np.arange(length)
    fourier = np.exp(-2j * np.pi * (index[:, None] * index[None, :] % length) / length)
    frequency = np.where(index < length // 2, index, index - length).astype(np.float64)
    phase = np.exp(-1j * np.pi * frequency**2 / (4 * length))
    fresnel = (np.conj(fourier) * phase[None, :]) @ fourier / length
    odd = 2 * index + 1
    turn = odd[:, None] * odd[None, :] % (4 * length)
    shifted = np.exp(-2j * np.pi * turn / (4 * length)) / np.sqrt(length)
    tables = []
    for matrix in (fresnel, shifted):
        for block in folded(matrix):
            for form in (left_form(block), left_form(np.conj(block))):
                tables.append(np.stack(split_table(form)))
    order = np.concatenate([index[: length // 2], index[length // 2 :][::-1]])
    ramp = np.exp(1j * np.pi * order / length)
    tilt = ramp[:, None] * ramp[None, :]
    return np.stack(tables), np.stack([tilt.real, tilt.imag]).astype(np.float32)


def reversal(size):
    row = lax.broadcasted_iota(jnp.int32, (size, size), 0)
    col = lax.broadcasted_iota(jnp.int32, (size, size), 1)
    return jnp.where(row + col == size - 1, 1.0, 0.0).astype(BF16)


def exact_dot(a, b):
    moving, table = (a, b) if b.dtype == BF16 else (b, a)
    total = None
    for part in range(3):
        piece = moving.astype(BF16)
        moving = moving - piece.astype(F32)
        done = jnp.dot(*((piece, b) if b.dtype == BF16 else (a, piece)), preferred_element_type=F32)
        total = done if total is None else total + done
    return total


def mirror_halves(fields, flip):
    count, size = len(fields), fields[0].shape[0]
    half = size // 2
    right = exact_dot(jnp.concatenate([x[:, half:] for x in fields], axis=0), flip)
    fields = [
        jnp.concatenate([x[:, :half], right[i * size : (i + 1) * size]], axis=1) for i, x in enumerate(fields)
    ]
    lower = exact_dot(flip, jnp.concatenate([x[half:] for x in fields], axis=1))
    return [
        jnp.concatenate([x[:half], lower[:, i * size : (i + 1) * size]], axis=0) for i, x in enumerate(fields)
    ]


def prep_kernel(ids, probe, amplitudes, probe_out, amp_out):
    flip = reversal(probe.shape[-1] // 2)
    probe_out[0], probe_out[1], amp_out[...] = mirror_halves([probe[0], probe[1], amplitudes[ids[0]]], flip)


def crop_kernel(peers, plane, waits, ids, positions, strips, rim, *rest):
    rest = rest[waits:]
    own_out, near_out = rest[:2]
    far_outs, rest = rest[2 : peers // 2 + 1], rest[peers // 2 + 1 :]
    outs = [own_out, near_out] + [far.at[i] for far in far_outs for i in range(2)]
    ext, cut, loaded, stored = rest
    rows, cols = rim.shape
    blocks = cols // LANES
    size = own_out.shape[-1]
    loads = []
    for block in range(blocks):
        columns = pl.ds(block * LANES, LANES)
        loads.append(
            pltpu.make_async_copy(
                strips.at[plane[0], plane[1], :, columns], ext.at[block, pl.ds(0, rows)], loaded.at[2 * block]
            )
        )
        loads.append(
            pltpu.make_async_copy(
                rim.at[:, columns], ext.at[block, pl.ds(rows, rows)], loaded.at[2 * block + 1]
            )
        )
    for copy in loads:
        copy.start()
    flip = reversal(size // 2)
    lane = lax.broadcasted_iota(jnp.int32, (size, LANES), 1)
    ext[blocks] = jnp.zeros((2 * rows, LANES), F32)
    for copy in loads:
        copy.wait()
    stores = []
    for pair in sorted(range(0, peers, 2), reverse=True):
        fields = []
        for offset in (pair, pair + 1):
            window = ids[0] ^ offset
            row_first = positions[window, 0] - ids[1] * rows
            col_first = positions[window, 1]
            block_first = col_first >> 7
            within = col_first & (LANES - 1)
            moved = [
                pltpu.roll(
                    ext[block_first + i, pl.ds(row_first, size), :], (LANES - within) & (LANES - 1), 1
                )
                for i in range(size // LANES + 1)
            ]
            keep = lane < LANES - within
            picked = [jnp.where(keep, moved[i], moved[i + 1]) for i in range(size // LANES)]
            fields.append(jnp.concatenate(picked, axis=1))
        fields = mirror_halves(fields, flip)
        for i, offset in enumerate((pair, pair + 1)):
            cut[offset] = fields[i]
            copy = pltpu.make_async_copy(cut.at[offset], outs[offset], stored.at[offset])
            copy.start()
            stores.append(copy)
    for copy in stores:
        copy.wait()


def strip_kernel(planes, waits, strips, *rest):
    outs = rest[waits : waits + len(planes)]
    held, moved = rest[waits + len(planes) :]
    loads, stores = [], []
    for i, plane in enumerate(planes):
        loads.append(pltpu.make_async_copy(strips.at[plane[0], plane[1]], held.at[i], moved.at[i]))
        stores.append(pltpu.make_async_copy(held.at[i], outs[i], moved.at[i]))
    for copy in loads:
        copy.start()
    for load, store in zip(loads, stores):
        load.wait()
        store.start()
    for copy in stores:
        copy.wait()


def place_kernel(peers, waits, ids, positions, *rest):
    own_in, near_in = rest[:2]
    far_ins = rest[2:peers]
    pieces = [own_in, near_in]
    for i in range(0, len(far_ins), 2):
        pieces += [far_ins[i].at[0], far_ins[i + 1]]
    own, rim, ext, got, loaded, stored = rest[peers + waits :]
    rows, cols = own.shape
    blocks = cols // LANES
    size = own_in.shape[-1]
    loads = [
        pltpu.make_async_copy(pieces[offset], got.at[offset], loaded.at[offset]) for offset in range(peers)
    ]
    for copy in loads:
        copy.start()
    flip = reversal(size // 2)
    lane = lax.broadcasted_iota(jnp.int32, (size, LANES), 1)
    ext[...] = jnp.zeros(ext.shape, F32)
    for copy in loads:
        copy.wait()
    fields = mirror_halves([got[offset] for offset in range(peers)], flip)
    for offset in range(peers):
        window = ids[0] ^ offset
        row_first = positions[window, 0] - ids[1] * rows
        col_first = positions[window, 1]
        block_first = col_first >> 7
        within = col_first & (LANES - 1)
        moved = [
            pltpu.roll(fields[offset][:, i * LANES : (i + 1) * LANES], within, 1) for i in range(size // LANES)
        ]
        keep = lane >= within
        zero = jnp.zeros((size, LANES), F32)
        moved = [zero] + moved + [zero]
        for i in range(size // LANES + 1):
            place = (block_first + i, pl.ds(row_first, size))
            ext[place] = ext[place] + jnp.where(keep, moved[i + 1], moved[i])
    stores = []
    for block in range(blocks):
        columns = pl.ds(block * LANES, LANES)
        stores.append(
            pltpu.make_async_copy(ext.at[block, pl.ds(rows, rows)], rim.at[:, columns], stored.at[2 * block])
        )
        stores.append(
            pltpu.make_async_copy(ext.at[block, pl.ds(0, rows)], own.at[:, columns], stored.at[2 * block + 1])
        )
    for copy in stores:
        copy.start()
    for copy in stores:
        copy.wait()


def split_value(x):
    high = x.astype(BF16)
    low = (x - high.astype(F32)).astype(BF16)
    return high, low


def dot32(a, b):
    return jnp.dot(a, b, preferred_element_type=F32)


def sandwich(re, im, tables, base, conj):
    half = re.shape[0] // 2

    def fold(x):
        upper, lower = x[:half], x[half:]
        even, odd = upper + lower, upper - lower
        parts = []
        for y in (even, odd):
            near, far = y[:, :half], y[:, half:]
            parts.append((near + far, near - far))
        return parts

    re_parts, im_parts = fold(re), fold(im)
    middle = []
    for b in range(2):
        field = jnp.concatenate(
            [jnp.concatenate([re_parts[a][b], im_parts[a][b]], axis=1) for a in range(2)], axis=0
        )
        high, low = split_value(field)
        middle.append(
            dot32(high, tables[base + 2 * b + 1 - conj, 0])
            + dot32(low, tables[base + 2 * b + 1 - conj, 0])
            + dot32(high, tables[base + 2 * b + 1 - conj, 1])
        )
    done = []
    for a in range(2):
        rows = slice(a * half, (a + 1) * half)
        field = jnp.concatenate(
            [
                jnp.concatenate([middle[b][rows, :half] for b in range(2)], axis=1),
                jnp.concatenate([middle[b][rows, half:] for b in range(2)], axis=1),
            ],
            axis=0,
        )
        high, low = split_value(field)
        done.append(
            dot32(tables[base + 2 * a + conj, 0], high)
            + dot32(tables[base + 2 * a + conj, 0], low)
            + dot32(tables[base + 2 * a + conj, 1], high)
        )

    def unfold(even, odd):
        rows = jnp.concatenate([even + odd, even - odd], axis=0)
        near, far = rows[:, :half], rows[:, half:]
        return jnp.concatenate([near + far, near - far], axis=1)

    return (
        unfold(done[0][:half], done[1][:half]),
        unfold(done[0][half:], done[1][half:]),
    )


def optics_kernel(peers, per_device, ids, probe_in, amplitude_in, tables_in, tilt_in, *rest):
    chunks = 2 * per_device
    groups = peers // 2 + 1
    crops, pieces = [], []
    for chunk in range(chunks):
        got = rest[chunk * peers : (chunk + 1) * peers]
        crops += list(got[:2])
        for i in range(2, peers, 2):
            crops += [got[i].at[0], got[i + 1]]
    rest = rest[chunks * peers :]
    for chunk in range(chunks):
        out = rest[chunk * groups : (chunk + 1) * groups]
        pieces += list(out[:2])
        for far in out[2:]:
            pieces += [far.at[0], far.at[1]]
    kept, handed = rest[chunks * groups : chunks * groups + 2]
    rest = rest[chunks * groups + 2 :]
    trans, history, terms, grad, tables, tilt, amplitude, fixed, loaded, stored = rest
    size = grad.shape[-1]
    share = size // peers
    layers = peers * per_device
    me = ids[0]
    half = tables.shape[0] // 2
    settings = [
        pltpu.make_async_copy(probe_in, history.at[0], fixed.at[0]),
        pltpu.make_async_copy(tables_in.at[pl.ds(0, half)], tables.at[pl.ds(0, half)], fixed.at[1]),
        pltpu.make_async_copy(tables_in.at[pl.ds(half, half)], tables.at[pl.ds(half, half)], fixed.at[2]),
        pltpu.make_async_copy(tilt_in, tilt, fixed.at[3]),
        pltpu.make_async_copy(amplitude_in, amplitude, fixed.at[4]),
    ]
    for copy in settings[:2]:
        copy.start()
    for j in range(per_device):
        for offset in range(peers):
            at = (me ^ offset) * per_device + j
            for part in range(2):
                pltpu.make_async_copy(
                    crops[(j * 2 + part) * peers + offset], trans.at[at, part], loaded.at[2 * at + part]
                ).start()
    for copy in settings[2:]:
        copy.start()
    for copy in settings[:2]:
        copy.wait()

    def mixed(layer):
        for part in range(2):
            pltpu.make_async_copy(crops[0], trans.at[layer, part], loaded.at[2 * layer + part]).wait()
        t_re, t_im = trans[layer, 0], trans[layer, 1]
        w_re, w_im = history[layer, 0], history[layer, 1]
        return t_re * w_re - t_im * w_im, t_re * w_im + t_im * w_re

    def forward(layer, carry):
        re, im = mixed(layer)
        re, im = sandwich(re, im, tables, 0, 0)
        history[layer + 1, 0] = re
        history[layer + 1, 1] = im
        return carry

    lax.fori_loop(0, layers - 1, forward, 0)
    re, im = mixed(layers - 1)
    for copy in settings[2:]:
        copy.wait()
    d_re, d_im = tilt[0], tilt[1]
    re, im = re * d_re - im * d_im, re * d_im + im * d_re
    re, im = sandwich(re, im, tables, 4, 0)
    factor = 1.0 - amplitude[...] / jnp.sqrt(re * re + im * im + 1.0)
    re, im = sandwich(re * factor, im * factor, tables, 4, 1)
    back_re, back_im = re * d_re + im * d_im, im * d_re - re * d_im

    def collect(layer, back_re, back_im):
        w_re, w_im = history[layer, 0], history[layer, 1]
        terms[layer, 0] = w_re * back_re + w_im * back_im
        terms[layer, 1] = w_re * back_im - w_im * back_re
        owner, j_now = lax.div(layer, per_device), lax.rem(layer, per_device)
        for j in range(per_device):
            for offset in range(peers):

                @pl.when((owner == me ^ offset) & (j_now == j))
                def _():
                    for part in range(2):
                        pltpu.make_async_copy(
                            terms.at[layer, part],
                            pieces[(j * 2 + part) * peers + offset].at[pl.ds(0, size)],
                            stored.at[2 * layer + part],
                        ).start()

        t_re, t_im = trans[layer, 0], trans[layer, 1]
        grad[0] = t_re * back_re + t_im * back_im
        grad[1] = t_re * back_im - t_im * back_re

    collect(layers - 1, back_re, back_im)

    def backward(step, carry):
        back_re, back_im = sandwich(grad[0], grad[1], tables, 0, 1)
        collect(layers - 2 - step, back_re, back_im)
        return carry

    lax.fori_loop(0, layers - 1, backward, 0)
    grad[0], grad[1] = mirror_halves([grad[0], grad[1]], reversal(size // 2))
    shares = []
    for offset in range(peers):
        first = pl.multiple_of((me ^ offset) * share, share)
        for part in range(2):
            shares.append(
                pltpu.make_async_copy(
                    grad.at[part, pl.ds(first, share)],
                    (kept, handed)[offset % 2].at[offset // 2, part],
                    fixed.at[2 * offset + part],
                )
            )
    for copy in shares:
        copy.start()
    for layer in range(layers):
        for part in range(2):
            pltpu.make_async_copy(
                terms.at[layer, part], pieces[0].at[pl.ds(0, size)], stored.at[2 * layer + part]
            ).wait()
    for copy in shares:
        copy.wait()


SMEM_SPEC = pl.BlockSpec(memory_space=pltpu.SMEM)
VMEM_SPEC = pl.BlockSpec(memory_space=pltpu.VMEM)
HBM_SPEC = pl.BlockSpec(memory_space=pltpu.HBM)


def gate_kernel(*refs):
    pass


def gate(passed, waits):
    total = len(passed)
    if not total or not waits:
        return passed
    return run_kernel(
        gate_kernel,
        "gate",
        tuple(shape(*x.shape) for x in passed),
        [HBM_SPEC] * (total + len(waits)),
        (HBM_SPEC,) * total,
        [],
        0.1,
        aliases={i: i for i in range(total)},
    )(*passed, *waits)


def run_kernel(kernel, name, out_shapes, in_specs, out_specs, scratch, micros, mebibytes=16, aliases={}):
    return pl.pallas_call(
        kernel,
        name=name,
        out_shape=out_shapes,
        in_specs=in_specs,
        out_specs=out_specs,
        scratch_shapes=scratch,
        input_output_aliases=aliases,
        compiler_params=pltpu.CompilerParams(vmem_limit_bytes=mebibytes * 2**20),
        cost_estimate=pl.CostEstimate(
            flops=int(micros * 1e6), bytes_accessed=int(micros * 1e3), transcendentals=0
        ),
    )


def shape(*dims):
    return jax.ShapeDtypeStruct(dims, F32)


def swap(x, axis, offset):
    peers = lax.axis_size(axis)
    return lax.ppermute(x, axis, [(i, i ^ offset) for i in range(peers)])


def exchanged(mine, waits=()):
    got = [mine[0], swap(mine[1], "depth", 1)]
    for i, pair in enumerate(mine[2:]):
        across = swap(pair, "depth", 2 * (i + 1))
        (across,) = gate([across], waits)
        got += [across, swap(across[1], "depth", 1)]
    return got


def echo(x):
    return swap(x[:8, :LANES], "depth", 1)


def shift(x, axis, by):
    peers = lax.axis_size(axis)
    return lax.ppermute(x, axis, [(i, i + by) for i in range(peers) if 0 <= i + by < peers])


def body(transmission, probe_field, scan_positions, amplitudes):
    size = probe_field.shape[-1]
    per_device, _, rows, cols = transmission.shape
    peers = lax.axis_size("depth")
    tiles = lax.axis_size("tile")
    ids = jnp.stack([lax.axis_index("depth"), lax.axis_index("tile")]).astype(jnp.int32)
    tables, tilt = (jnp.asarray(x) for x in optics_tables(size))

    probe, amplitude = run_kernel(
        prep_kernel,
        "prep",
        (shape(2, size, size), shape(size, size)),
        [SMEM_SPEC, VMEM_SPEC, VMEM_SPEC],
        [VMEM_SPEC, VMEM_SPEC],
        [],
        2,
    )(ids, probe_field, amplitudes)

    chunks = [(j, part) for j in range(per_device) for part in range(2)]
    ahead = 2

    def strips_of(planes, waits):
        return run_kernel(
            functools.partial(strip_kernel, planes, len(waits)),
            "strip",
            (shape(rows, cols),) * len(planes),
            [HBM_SPEC] * (1 + len(waits)),
            (HBM_SPEC,) * len(planes),
            [pltpu.VMEM((len(planes), rows, cols), F32), pltpu.SemaphoreType.DMA((len(planes),))],
            1,
            56,
        )(transmission, *waits)

    strips = list(strips_of(chunks[:1], []))
    strips += strips_of(chunks[1:], strips[:1])
    group = (shape(size, size),) * 2 + (shape(2, size, size),) * (peers // 2 - 1)
    groups = len(group)
    crops = []
    for k, c in enumerate(chunks):
        rim = shift(strips[k], "tile", -1)
        waits = crops[k - ahead][2::2] if k >= ahead else [probe, amplitude]
        mine = run_kernel(
            functools.partial(crop_kernel, peers, c, len(waits)),
            "crop",
            group,
            [SMEM_SPEC, SMEM_SPEC] + [HBM_SPEC] * (2 + len(waits)),
            (HBM_SPEC,) * groups,
            [
                pltpu.VMEM((cols // LANES + 1, 2 * rows, LANES), F32),
                pltpu.VMEM((peers, size, size), F32),
                pltpu.SemaphoreType.DMA((2 * cols // LANES,)),
                pltpu.SemaphoreType.DMA((peers,)),
            ],
            2,
        )(ids, scan_positions, transmission, rim, *waits)
        strips[k + ahead : k + ahead + 1] = gate(strips[k + ahead : k + ahead + 1], mine[:1])
        early = [x for got in crops[:-1] for x in got[1:2] + got[3::2]] if k == len(chunks) - 1 else []
        crops.append(exchanged(mine, early))
    layers = per_device * peers
    result = run_kernel(
        functools.partial(optics_kernel, peers, per_device),
        "optics",
        group * len(chunks) + (shape(peers // 2, 2, size // peers, size),) * 2,
        [SMEM_SPEC] + [HBM_SPEC] * (4 + len(chunks) * peers),
        (HBM_SPEC,) * (len(chunks) * groups + 2),
        [
            pltpu.VMEM((layers, 2, size, size), F32),
            pltpu.VMEM((layers, 2, size, size), F32),
            pltpu.VMEM((layers, 2, size, size), F32),
            pltpu.VMEM((2, size, size), F32),
            pltpu.VMEM(tables.shape, BF16),
            pltpu.VMEM(tilt.shape, F32),
            pltpu.VMEM((size, size), F32),
            pltpu.SemaphoreType.DMA((max(5, 2 * peers),)),
            pltpu.SemaphoreType.DMA((2 * layers,)),
            pltpu.SemaphoreType.DMA((2 * layers,)),
        ],
        15,
        32,
    )(ids, probe, amplitude, tables, tilt, *[x for got in crops for x in got])

    kept, handed = result[-2:]
    probe_halves = kept + swap(handed, "depth", 1)
    probe_grad = probe_halves
    step = 2
    while step < peers:
        probe_grad = probe_grad[:1] + swap(probe_grad[1:], "depth", step)
        step *= 2
    probe_steps = [probe_grad[0]]
    step = tiles // 2
    while step:
        probe_steps.append(probe_steps[-1] + swap(probe_steps[-1], "tile", step))
        step //= 2

    own, rim_back, returned = {}, {}, []
    order = list(reversed(chunks))
    for k, c in enumerate(order):
        at = chunks.index(c) * groups
        mine = result[at : at + groups]
        if k == 0:
            mine = gate(mine, [probe_steps[0]])
        if k >= ahead:
            mine = gate(mine, returned[k - ahead][2::2] + [own[order[k - ahead]]])
        before = [own[order[k - 1]]] if k else probe_steps[-2:-1]
        if k >= ahead:
            before.append(rim_back[order[k - ahead]])
        returned.append(exchanged(mine, before))
        waits = [swap(probe_steps[-1], "depth", 1)] if k == 1 else []
        mine = run_kernel(
            functools.partial(place_kernel, peers, len(waits)),
            "place",
            (shape(rows, cols), shape(rows, cols)),
            [SMEM_SPEC, SMEM_SPEC] + [HBM_SPEC] * (peers + len(waits)),
            (HBM_SPEC, HBM_SPEC),
            [
                pltpu.VMEM((cols // LANES + 1, 2 * rows, LANES), F32),
                pltpu.VMEM((peers, size, size), F32),
                pltpu.SemaphoreType.DMA((peers,)),
                pltpu.SemaphoreType.DMA((2 * cols // LANES,)),
            ],
            2,
        )(ids, scan_positions, *returned[k], *waits)
        own[c], outside = mine[:2]
        if k >= ahead:
            (outside,) = gate([outside], [echo(echo(rim_back[order[k - ahead]]))])
        rim_back[c] = shift(outside, "tile", 1)

    rim_back[order[-2]] = gate([rim_back[order[-2]]], [echo(rim_back[order[-2]])])[0]
    object_grad = jnp.stack(
        [
            jnp.stack([own[(j, part)] + rim_back[(j, part)] for part in range(2)])
            for j in range(per_device)
        ]
    )
    return (object_grad, probe_steps[-1])


def solution(mesh):
    placed = (P("depth", None, "tile", None), P(), P("tile", None), P("tile", None, None))
    return jax.shard_map(
        body,
        mesh=mesh,
        in_specs=placed,
        out_specs=(P("depth", None, "tile", None), P(None, "depth", None)),
        check_vma=False,
    )
```

```python
import functools

import jax
import jax.numpy as jnp
import ml_dtypes
import numpy as np
from jax import lax
from jax.experimental import pallas as pl
from jax.experimental.pallas import tpu as pltpu
from jax.sharding import PartitionSpec as P

LANES = 128
F32 = jnp.float32
BF16 = jnp.bfloat16


def split_table(table):
    high = table.astype(np.float32).astype(ml_dtypes.bfloat16)
    low = (table - high.astype(np.float64)).astype(np.float32).astype(ml_dtypes.bfloat16)
    return high, low


def left_form(matrix):
    return np.block([[matrix.real, -matrix.imag], [matrix.imag, matrix.real]])


def folded(matrix):
    half = matrix.shape[0] // 2
    near = matrix[:half, :half]
    mirrored = matrix[:half, half:][:, ::-1]
    return (near + mirrored) / 2, (near - mirrored) / 2


def optics_tables(length):
    index = np.arange(length)
    fourier = np.exp(-2j * np.pi * (index[:, None] * index[None, :] % length) / length)
    frequency = np.where(index < length // 2, index, index - length).astype(np.float64)
    phase = np.exp(-1j * np.pi * frequency**2 / (4 * length))
    fresnel = (np.conj(fourier) * phase[None, :]) @ fourier / length
    odd = 2 * index + 1
    turn = odd[:, None] * odd[None, :] % (4 * length)
    shifted = np.exp(-2j * np.pi * turn / (4 * length)) / np.sqrt(length)
    tables = []
    for matrix in (fresnel, shifted):
        for block in folded(matrix):
            for form in (left_form(block), left_form(np.conj(block))):
                tables.append(np.stack(split_table(form)))
    order = np.concatenate([index[: length // 2], index[length // 2 :][::-1]])
    ramp = np.exp(1j * np.pi * order / length)
    tilt = ramp[:, None] * ramp[None, :]
    return np.stack(tables), np.stack([tilt.real, tilt.imag]).astype(np.float32)


def reversal(size):
    row = lax.broadcasted_iota(jnp.int32, (size, size), 0)
    col = lax.broadcasted_iota(jnp.int32, (size, size), 1)
    return jnp.where(row + col == size - 1, 1.0, 0.0).astype(BF16)


def exact_dot(a, b):
    moving, table = (a, b) if b.dtype == BF16 else (b, a)
    total = None
    for part in range(3):
        piece = moving.astype(BF16)
        moving = moving - piece.astype(F32)
        done = jnp.dot(*((piece, b) if b.dtype == BF16 else (a, piece)), preferred_element_type=F32)
        total = done if total is None else total + done
    return total


def mirror_halves(fields, flip):
    count, size = len(fields), fields[0].shape[0]
    half = size // 2
    right = exact_dot(jnp.concatenate([x[:, half:] for x in fields], axis=0), flip)
    fields = [
        jnp.concatenate([x[:, :half], right[i * size : (i + 1) * size]], axis=1) for i, x in enumerate(fields)
    ]
    lower = exact_dot(flip, jnp.concatenate([x[half:] for x in fields], axis=1))
    return [
        jnp.concatenate([x[:half], lower[:, i * size : (i + 1) * size]], axis=0) for i, x in enumerate(fields)
    ]


def prep_kernel(ids, probe, amplitudes, probe_out, amp_out):
    flip = reversal(probe.shape[-1] // 2)
    probe_out[0], probe_out[1], amp_out[...] = mirror_halves([probe[0], probe[1], amplitudes[ids[0]]], flip)


def crop_kernel(peers, plane, waits, ids, positions, strips, rim, *rest):
    rest = rest[waits:]
    own_out, near_out = rest[:2]
    far_outs, rest = rest[2 : peers // 2 + 1], rest[peers // 2 + 1 :]
    outs = [own_out, near_out] + [far.at[i] for far in far_outs for i in range(2)]
    ext, cut, loaded, stored = rest
    rows, cols = rim.shape
    blocks = cols // LANES
    size = own_out.shape[-1]
    loads = []
    for block in range(blocks):
        columns = pl.ds(block * LANES, LANES)
        loads.append(
            pltpu.make_async_copy(
                strips.at[plane[0], plane[1], :, columns], ext.at[block, pl.ds(0, rows)], loaded.at[2 * block]
            )
        )
        loads.append(
            pltpu.make_async_copy(
                rim.at[:, columns], ext.at[block, pl.ds(rows, rows)], loaded.at[2 * block + 1]
            )
        )
    for copy in loads:
        copy.start()
    flip = reversal(size // 2)
    lane = lax.broadcasted_iota(jnp.int32, (size, LANES), 1)
    ext[blocks] = jnp.zeros((2 * rows, LANES), F32)
    for copy in loads:
        copy.wait()
    stores = []
    for pair in sorted(range(0, peers, 2), reverse=True):
        fields = []
        for offset in (pair, pair + 1):
            window = ids[0] ^ offset
            row_first = positions[window, 0] - ids[1] * rows
            col_first = positions[window, 1]
            block_first = col_first >> 7
            within = col_first & (LANES - 1)
            moved = [
                pltpu.roll(
                    ext[block_first + i, pl.ds(row_first, size), :], (LANES - within) & (LANES - 1), 1
                )
                for i in range(size // LANES + 1)
            ]
            keep = lane < LANES - within
            picked = [jnp.where(keep, moved[i], moved[i + 1]) for i in range(size // LANES)]
            fields.append(jnp.concatenate(picked, axis=1))
        fields = mirror_halves(fields, flip)
        for i, offset in enumerate((pair, pair + 1)):
            cut[offset] = fields[i]
            copy = pltpu.make_async_copy(cut.at[offset], outs[offset], stored.at[offset])
            copy.start()
            stores.append(copy)
    for copy in stores:
        copy.wait()


def strip_kernel(planes, waits, strips, *rest):
    outs = rest[waits : waits + len(planes)]
    held, moved = rest[waits + len(planes) :]
    loads, stores = [], []
    for i, plane in enumerate(planes):
        loads.append(pltpu.make_async_copy(strips.at[plane[0], plane[1]], held.at[i], moved.at[i]))
        stores.append(pltpu.make_async_copy(held.at[i], outs[i], moved.at[i]))
    for copy in loads:
        copy.start()
    for load, store in zip(loads, stores):
        load.wait()
        store.start()
    for copy in stores:
        copy.wait()


def place_kernel(peers, waits, ids, positions, *rest):
    own_in, near_in = rest[:2]
    far_ins = rest[2:peers]
    pieces = [own_in, near_in]
    for i in range(0, len(far_ins), 2):
        pieces += [far_ins[i].at[0], far_ins[i + 1]]
    own, rim, ext, got, loaded, stored = rest[peers + waits :]
    rows, cols = own.shape
    blocks = cols // LANES
    size = own_in.shape[-1]
    loads = [
        pltpu.make_async_copy(pieces[offset], got.at[offset], loaded.at[offset]) for offset in range(peers)
    ]
    for copy in loads:
        copy.start()
    flip = reversal(size // 2)
    lane = lax.broadcasted_iota(jnp.int32, (size, LANES), 1)
    ext[...] = jnp.zeros(ext.shape, F32)
    for copy in loads:
        copy.wait()
    fields = mirror_halves([got[offset] for offset in range(peers)], flip)
    for offset in range(peers):
        window = ids[0] ^ offset
        row_first = positions[window, 0] - ids[1] * rows
        col_first = positions[window, 1]
        block_first = col_first >> 7
        within = col_first & (LANES - 1)
        moved = [
            pltpu.roll(fields[offset][:, i * LANES : (i + 1) * LANES], within, 1) for i in range(size // LANES)
        ]
        keep = lane >= within
        zero = jnp.zeros((size, LANES), F32)
        moved = [zero] + moved + [zero]
        for i in range(size // LANES + 1):
            place = (block_first + i, pl.ds(row_first, size))
            ext[place] = ext[place] + jnp.where(keep, moved[i + 1], moved[i])
    stores = []
    for block in range(blocks):
        columns = pl.ds(block * LANES, LANES)
        stores.append(
            pltpu.make_async_copy(ext.at[block, pl.ds(rows, rows)], rim.at[:, columns], stored.at[2 * block])
        )
        stores.append(
            pltpu.make_async_copy(ext.at[block, pl.ds(0, rows)], own.at[:, columns], stored.at[2 * block + 1])
        )
    for copy in stores:
        copy.start()
    for copy in stores:
        copy.wait()


def split_value(x):
    high = x.astype(BF16)
    low = (x - high.astype(F32)).astype(BF16)
    return high, low


def dot32(a, b):
    return jnp.dot(a, b, preferred_element_type=F32)


def sandwich(re, im, tables, base, conj):
    half = re.shape[0] // 2

    def fold(x):
        upper, lower = x[:half], x[half:]
        even, odd = upper + lower, upper - lower
        parts = []
        for y in (even, odd):
            near, far = y[:, :half], y[:, half:]
            parts.append((near + far, near - far))
        return parts

    re_parts, im_parts = fold(re), fold(im)
    middle = []
    for b in range(2):
        field = jnp.concatenate(
            [jnp.concatenate([re_parts[a][b], im_parts[a][b]], axis=1) for a in range(2)], axis=0
        )
        high, low = split_value(field)
        middle.append(
            dot32(high, tables[base + 2 * b + 1 - conj, 0])
            + dot32(low, tables[base + 2 * b + 1 - conj, 0])
            + dot32(high, tables[base + 2 * b + 1 - conj, 1])
        )
    done = []
    for a in range(2):
        rows = slice(a * half, (a + 1) * half)
        field = jnp.concatenate(
            [
                jnp.concatenate([middle[b][rows, :half] for b in range(2)], axis=1),
                jnp.concatenate([middle[b][rows, half:] for b in range(2)], axis=1),
            ],
            axis=0,
        )
        high, low = split_value(field)
        done.append(
            dot32(tables[base + 2 * a + conj, 0], high)
            + dot32(tables[base + 2 * a + conj, 0], low)
            + dot32(tables[base + 2 * a + conj, 1], high)
        )

    def unfold(even, odd):
        rows = jnp.concatenate([even + odd, even - odd], axis=0)
        near, far = rows[:, :half], rows[:, half:]
        return jnp.concatenate([near + far, near - far], axis=1)

    return (
        unfold(done[0][:half], done[1][:half]),
        unfold(done[0][half:], done[1][half:]),
    )


def optics_kernel(peers, per_device, ids, probe_in, amplitude_in, tables_in, tilt_in, *rest):
    chunks = 2 * per_device
    groups = peers // 2 + 1
    crops, pieces = [], []
    for chunk in range(chunks):
        got = rest[chunk * peers : (chunk + 1) * peers]
        crops += list(got[:2])
        for i in range(2, peers, 2):
            crops += [got[i].at[0], got[i + 1]]
    rest = rest[chunks * peers :]
    for chunk in range(chunks):
        out = rest[chunk * groups : (chunk + 1) * groups]
        pieces += list(out[:2])
        for far in out[2:]:
            pieces += [far.at[0], far.at[1]]
    kept, handed = rest[chunks * groups : chunks * groups + 2]
    rest = rest[chunks * groups + 2 :]
    trans, history, terms, grad, tables, tilt, amplitude, fixed, loaded, stored = rest
    size = grad.shape[-1]
    share = size // peers
    layers = peers * per_device
    me = ids[0]
    half = tables.shape[0] // 2
    settings = [
        pltpu.make_async_copy(probe_in, history.at[0], fixed.at[0]),
        pltpu.make_async_copy(tables_in.at[pl.ds(0, half)], tables.at[pl.ds(0, half)], fixed.at[1]),
        pltpu.make_async_copy(tables_in.at[pl.ds(half, half)], tables.at[pl.ds(half, half)], fixed.at[2]),
        pltpu.make_async_copy(tilt_in, tilt, fixed.at[3]),
        pltpu.make_async_copy(amplitude_in, amplitude, fixed.at[4]),
    ]
    for copy in settings[:2]:
        copy.start()
    for j in range(per_device):
        for offset in range(peers):
            at = (me ^ offset) * per_device + j
            for part in range(2):
                pltpu.make_async_copy(
                    crops[(j * 2 + part) * peers + offset], trans.at[at, part], loaded.at[2 * at + part]
                ).start()
    for copy in settings[2:]:
        copy.start()
    for copy in settings[:2]:
        copy.wait()

    def mixed(layer):
        for part in range(2):
            pltpu.make_async_copy(crops[0], trans.at[layer, part], loaded.at[2 * layer + part]).wait()
        t_re, t_im = trans[layer, 0], trans[layer, 1]
        w_re, w_im = history[layer, 0], history[layer, 1]
        return t_re * w_re - t_im * w_im, t_re * w_im + t_im * w_re

    def forward(layer, carry):
        re, im = mixed(layer)
        re, im = sandwich(re, im, tables, 0, 0)
        history[layer + 1, 0] = re
        history[layer + 1, 1] = im
        return carry

    lax.fori_loop(0, layers - 1, forward, 0)
    re, im = mixed(layers - 1)
    for copy in settings[2:]:
        copy.wait()
    d_re, d_im = tilt[0], tilt[1]
    re, im = re * d_re - im * d_im, re * d_im + im * d_re
    re, im = sandwich(re, im, tables, 4, 0)
    factor = 1.0 - amplitude[...] / jnp.sqrt(re * re + im * im + 1.0)
    re, im = sandwich(re * factor, im * factor, tables, 4, 1)
    back_re, back_im = re * d_re + im * d_im, im * d_re - re * d_im

    def collect(layer, back_re, back_im):
        w_re, w_im = history[layer, 0], history[layer, 1]
        terms[layer, 0] = w_re * back_re + w_im * back_im
        terms[layer, 1] = w_re * back_im - w_im * back_re
        owner, j_now = lax.div(layer, per_device), lax.rem(layer, per_device)
        for j in range(per_device):
            for offset in range(peers):

                @pl.when((owner == me ^ offset) & (j_now == j))
                def _():
                    for part in range(2):
                        pltpu.make_async_copy(
                            terms.at[layer, part],
                            pieces[(j * 2 + part) * peers + offset].at[pl.ds(0, size)],
                            stored.at[2 * layer + part],
                        ).start()

        t_re, t_im = trans[layer, 0], trans[layer, 1]
        grad[0] = t_re * back_re + t_im * back_im
        grad[1] = t_re * back_im - t_im * back_re

    collect(layers - 1, back_re, back_im)

    def backward(step, carry):
        back_re, back_im = sandwich(grad[0], grad[1], tables, 0, 1)
        collect(layers - 2 - step, back_re, back_im)
        return carry

    lax.fori_loop(0, layers - 1, backward, 0)
    grad[0], grad[1] = mirror_halves([grad[0], grad[1]], reversal(size // 2))
    shares = []
    for offset in range(peers):
        first = pl.multiple_of((me ^ offset) * share, share)
        for part in range(2):
            shares.append(
                pltpu.make_async_copy(
                    grad.at[part, pl.ds(first, share)],
                    (kept, handed)[offset % 2].at[offset // 2, part],
                    fixed.at[2 * offset + part],
                )
            )
    for copy in shares:
        copy.start()
    for layer in range(layers):
        for part in range(2):
            pltpu.make_async_copy(
                terms.at[layer, part], pieces[0].at[pl.ds(0, size)], stored.at[2 * layer + part]
            ).wait()
    for copy in shares:
        copy.wait()


SMEM_SPEC = pl.BlockSpec(memory_space=pltpu.SMEM)
VMEM_SPEC = pl.BlockSpec(memory_space=pltpu.VMEM)
HBM_SPEC = pl.BlockSpec(memory_space=pltpu.HBM)


def gate_kernel(*refs):
    pass


def gate(passed, waits):
    total = len(passed)
    if not total or not waits:
        return passed
    return run_kernel(
        gate_kernel,
        "gate",
        tuple(shape(*x.shape) for x in passed),
        [HBM_SPEC] * (total + len(waits)),
        (HBM_SPEC,) * total,
        [],
        0.1,
        aliases={i: i for i in range(total)},
    )(*passed, *waits)


def run_kernel(kernel, name, out_shapes, in_specs, out_specs, scratch, micros, mebibytes=16, aliases={}):
    return pl.pallas_call(
        kernel,
        name=name,
        out_shape=out_shapes,
        in_specs=in_specs,
        out_specs=out_specs,
        scratch_shapes=scratch,
        input_output_aliases=aliases,
        compiler_params=pltpu.CompilerParams(vmem_limit_bytes=mebibytes * 2**20),
        cost_estimate=pl.CostEstimate(
            flops=int(micros * 1e6), bytes_accessed=int(micros * 1e3), transcendentals=0
        ),
    )


def shape(*dims):
    return jax.ShapeDtypeStruct(dims, F32)


def swap(x, axis, offset):
    peers = lax.axis_size(axis)
    return lax.ppermute(x, axis, [(i, i ^ offset) for i in range(peers)])


def exchanged(mine, waits=()):
    got = [mine[0], swap(mine[1], "depth", 1)]
    for i, pair in enumerate(mine[2:]):
        across = swap(pair, "depth", 2 * (i + 1))
        (across,) = gate([across], waits)
        got += [across, swap(across[1], "depth", 1)]
    return got


def echo(x):
    return swap(x[:8, :LANES], "depth", 1)


def shift(x, axis, by):
    peers = lax.axis_size(axis)
    return lax.ppermute(x, axis, [(i, i + by) for i in range(peers) if 0 <= i + by < peers])


def body(transmission, probe_field, scan_positions, amplitudes):
    size = probe_field.shape[-1]
    per_device, _, rows, cols = transmission.shape
    peers = lax.axis_size("depth")
    tiles = lax.axis_size("tile")
    ids = jnp.stack([lax.axis_index("depth"), lax.axis_index("tile")]).astype(jnp.int32)
    tables, tilt = (jnp.asarray(x) for x in optics_tables(size))

    probe, amplitude = run_kernel(
        prep_kernel,
        "prep",
        (shape(2, size, size), shape(size, size)),
        [SMEM_SPEC, VMEM_SPEC, VMEM_SPEC],
        [VMEM_SPEC, VMEM_SPEC],
        [],
        2,
    )(ids, probe_field, amplitudes)

    chunks = [(j, part) for j in range(per_device) for part in range(2)]
    ahead = 2

    def strips_of(planes, waits):
        return run_kernel(
            functools.partial(strip_kernel, planes, len(waits)),
            "strip",
            (shape(rows, cols),) * len(planes),
            [HBM_SPEC] * (1 + len(waits)),
            (HBM_SPEC,) * len(planes),
            [pltpu.VMEM((len(planes), rows, cols), F32), pltpu.SemaphoreType.DMA((len(planes),))],
            1,
            56,
        )(transmission, *waits)

    strips = list(strips_of(chunks[:1], []))
    strips += strips_of(chunks[1:], strips[:1])
    strips[1:2] = gate(strips[1:2], [amplitude])
    group = (shape(size, size),) * 2 + (shape(2, size, size),) * (peers // 2 - 1)
    groups = len(group)
    crops = []
    for k, c in enumerate(chunks):
        rim = shift(strips[k], "tile", -1)
        waits = crops[k - ahead][2::2] if k >= ahead else [probe, amplitude]
        mine = run_kernel(
            functools.partial(crop_kernel, peers, c, len(waits)),
            "crop",
            group,
            [SMEM_SPEC, SMEM_SPEC] + [HBM_SPEC] * (2 + len(waits)),
            (HBM_SPEC,) * groups,
            [
                pltpu.VMEM((cols // LANES + 1, 2 * rows, LANES), F32),
                pltpu.VMEM((peers, size, size), F32),
                pltpu.SemaphoreType.DMA((2 * cols // LANES,)),
                pltpu.SemaphoreType.DMA((peers,)),
            ],
            2,
        )(ids, scan_positions, transmission, rim, *waits)
        strips[k + ahead : k + ahead + 1] = gate(strips[k + ahead : k + ahead + 1], mine[:1])
        early = [x for got in crops[:-1] for x in got[1:2] + got[3::2]] if k == len(chunks) - 1 else []
        crops.append(exchanged(mine, early))
    layers = per_device * peers
    result = run_kernel(
        functools.partial(optics_kernel, peers, per_device),
        "optics",
        group * len(chunks) + (shape(peers // 2, 2, size // peers, size),) * 2,
        [SMEM_SPEC] + [HBM_SPEC] * (4 + len(chunks) * peers),
        (HBM_SPEC,) * (len(chunks) * groups + 2),
        [
            pltpu.VMEM((layers, 2, size, size), F32),
            pltpu.VMEM((layers, 2, size, size), F32),
            pltpu.VMEM((layers, 2, size, size), F32),
            pltpu.VMEM((2, size, size), F32),
            pltpu.VMEM(tables.shape, BF16),
            pltpu.VMEM(tilt.shape, F32),
            pltpu.VMEM((size, size), F32),
            pltpu.SemaphoreType.DMA((max(5, 2 * peers),)),
            pltpu.SemaphoreType.DMA((2 * layers,)),
            pltpu.SemaphoreType.DMA((2 * layers,)),
        ],
        15,
        32,
    )(ids, probe, amplitude, tables, tilt, *[x for got in crops for x in got])

    kept, handed = result[-2:]
    probe_halves = kept + swap(handed, "depth", 1)
    probe_grad = probe_halves
    step = 2
    while step < peers:
        probe_grad = probe_grad[:1] + swap(probe_grad[1:], "depth", step)
        step *= 2
    probe_steps = [probe_grad[0]]
    step = tiles // 2
    while step:
        probe_steps.append(probe_steps[-1] + swap(probe_steps[-1], "tile", step))
        step //= 2

    own, rim_back, returned = {}, {}, []
    order = list(reversed(chunks))
    for k, c in enumerate(order):
        at = chunks.index(c) * groups
        mine = result[at : at + groups]
        if k == 0:
            mine = gate(mine, [probe_steps[0]])
        if k >= ahead:
            mine = gate(mine, returned[1][2::2] + [own[order[k - ahead]]])
        before = [own[order[k - 1]]] if k else probe_steps[-2:-1]
        if k == ahead:
            before.append(rim_back[order[k - ahead]])
        returned.append(exchanged(mine, before))
        waits = [swap(swap(probe_steps[-1], "depth", 1), "depth", 1)] if k == 1 else []
        mine = run_kernel(
            functools.partial(place_kernel, peers, len(waits)),
            "place",
            (shape(rows, cols), shape(rows, cols)),
            [SMEM_SPEC, SMEM_SPEC] + [HBM_SPEC] * (peers + len(waits)),
            (HBM_SPEC, HBM_SPEC),
            [
                pltpu.VMEM((cols // LANES + 1, 2 * rows, LANES), F32),
                pltpu.VMEM((peers, size, size), F32),
                pltpu.SemaphoreType.DMA((peers,)),
                pltpu.SemaphoreType.DMA((2 * cols // LANES,)),
            ],
            2,
        )(ids, scan_positions, *returned[k], *waits)
        own[c], outside = mine[:2]
        if k >= ahead:
            earlier = order[k - ahead]
            (rim_back[earlier],) = gate([rim_back[earlier]], [own[order[k - 1]]])
            (outside,) = gate([outside], [echo(echo(rim_back[order[k - ahead]]))])
        rim_back[c] = shift(outside, "tile", 1)

    rim_back[order[-2]] = gate([rim_back[order[-2]]], [swap(rim_back[order[-2]][: rows // 2], "depth", 1)])[0]
    object_grad = jnp.stack(
        [
            jnp.stack([own[(j, part)] + rim_back[(j, part)] for part in range(2)])
            for j in range(per_device)
        ]
    )
    return (object_grad, probe_steps[-1])


def solution(mesh):
    placed = (P("depth", None, "tile", None), P(), P("tile", None), P("tile", None, None))
    return jax.shard_map(
        body,
        mesh=mesh,
        in_specs=placed,
        out_specs=(P("depth", None, "tile", None), P(None, "depth", None)),
        check_vma=False,
    )
```

```python
import functools

import jax
import jax.numpy as jnp
import ml_dtypes
import numpy as np
from jax import lax
from jax.experimental import pallas as pl
from jax.experimental.pallas import tpu as pltpu
from jax.sharding import PartitionSpec as P

LANES = 128
F32 = jnp.float32
BF16 = jnp.bfloat16


def split_table(table):
    high = table.astype(np.float32).astype(ml_dtypes.bfloat16)
    low = (table - high.astype(np.float64)).astype(np.float32).astype(ml_dtypes.bfloat16)
    return high, low


def left_form(matrix):
    return np.block([[matrix.real, -matrix.imag], [matrix.imag, matrix.real]])


def folded(matrix):
    half = matrix.shape[0] // 2
    near = matrix[:half, :half]
    mirrored = matrix[:half, half:][:, ::-1]
    return (near + mirrored) / 2, (near - mirrored) / 2


def optics_tables(length):
    index = np.arange(length)
    fourier = np.exp(-2j * np.pi * (index[:, None] * index[None, :] % length) / length)
    frequency = np.where(index < length // 2, index, index - length).astype(np.float64)
    phase = np.exp(-1j * np.pi * frequency**2 / (4 * length))
    fresnel = (np.conj(fourier) * phase[None, :]) @ fourier / length
    odd = 2 * index + 1
    turn = odd[:, None] * odd[None, :] % (4 * length)
    shifted = np.exp(-2j * np.pi * turn / (4 * length)) / np.sqrt(length)
    tables = []
    for matrix in (fresnel, shifted):
        for block in folded(matrix):
            for form in (left_form(block), left_form(np.conj(block))):
                tables.append(np.stack(split_table(form)))
    order = np.concatenate([index[: length // 2], index[length // 2 :][::-1]])
    ramp = np.exp(1j * np.pi * order / length)
    tilt = ramp[:, None] * ramp[None, :]
    return np.stack(tables), np.stack([tilt.real, tilt.imag]).astype(np.float32)


def reversal(size):
    row = lax.broadcasted_iota(jnp.int32, (size, size), 0)
    col = lax.broadcasted_iota(jnp.int32, (size, size), 1)
    return jnp.where(row + col == size - 1, 1.0, 0.0).astype(BF16)


def exact_dot(a, b):
    moving, table = (a, b) if b.dtype == BF16 else (b, a)
    total = None
    for part in range(3):
        piece = moving.astype(BF16)
        moving = moving - piece.astype(F32)
        done = jnp.dot(*((piece, b) if b.dtype == BF16 else (a, piece)), preferred_element_type=F32)
        total = done if total is None else total + done
    return total


def mirror_halves(fields, flip):
    count, size = len(fields), fields[0].shape[0]
    half = size // 2
    right = exact_dot(jnp.concatenate([x[:, half:] for x in fields], axis=0), flip)
    fields = [
        jnp.concatenate([x[:, :half], right[i * size : (i + 1) * size]], axis=1) for i, x in enumerate(fields)
    ]
    lower = exact_dot(flip, jnp.concatenate([x[half:] for x in fields], axis=1))
    return [
        jnp.concatenate([x[:half], lower[:, i * size : (i + 1) * size]], axis=0) for i, x in enumerate(fields)
    ]


def prep_kernel(ids, probe, amplitudes, probe_out, amp_out):
    flip = reversal(probe.shape[-1] // 2)
    probe_out[0], probe_out[1], amp_out[...] = mirror_halves([probe[0], probe[1], amplitudes[ids[0]]], flip)


def crop_kernel(peers, plane, waits, ids, positions, strips, rim, *rest):
    rest = rest[waits:]
    own_out, near_out = rest[:2]
    far_outs, rest = rest[2 : peers // 2 + 1], rest[peers // 2 + 1 :]
    outs = [own_out, near_out] + [far.at[i] for far in far_outs for i in range(2)]
    ext, cut, loaded, stored = rest
    rows, cols = rim.shape
    blocks = cols // LANES
    size = own_out.shape[-1]
    loads = []
    for block in range(blocks):
        columns = pl.ds(block * LANES, LANES)
        loads.append(
            pltpu.make_async_copy(
                strips.at[plane[0], plane[1], :, columns], ext.at[block, pl.ds(0, rows)], loaded.at[2 * block]
            )
        )
        loads.append(
            pltpu.make_async_copy(
                rim.at[:, columns], ext.at[block, pl.ds(rows, rows)], loaded.at[2 * block + 1]
            )
        )
    for copy in loads:
        copy.start()
    flip = reversal(size // 2)
    lane = lax.broadcasted_iota(jnp.int32, (size, LANES), 1)
    ext[blocks] = jnp.zeros((2 * rows, LANES), F32)
    for copy in loads:
        copy.wait()
    stores = []
    for pair in sorted(range(0, peers, 2), reverse=True):
        fields = []
        for offset in (pair, pair + 1):
            window = ids[0] ^ offset
            row_first = positions[window, 0] - ids[1] * rows
            col_first = positions[window, 1]
            block_first = col_first >> 7
            within = col_first & (LANES - 1)
            moved = [
                pltpu.roll(
                    ext[block_first + i, pl.ds(row_first, size), :], (LANES - within) & (LANES - 1), 1
                )
                for i in range(size // LANES + 1)
            ]
            keep = lane < LANES - within
            picked = [jnp.where(keep, moved[i], moved[i + 1]) for i in range(size // LANES)]
            fields.append(jnp.concatenate(picked, axis=1))
        fields = mirror_halves(fields, flip)
        for i, offset in enumerate((pair, pair + 1)):
            cut[offset] = fields[i]
            copy = pltpu.make_async_copy(cut.at[offset], outs[offset], stored.at[offset])
            copy.start()
            stores.append(copy)
    for copy in stores:
        copy.wait()


def strip_kernel(planes, waits, strips, *rest):
    outs = rest[waits : waits + len(planes)]
    held, moved = rest[waits + len(planes) :]
    loads, stores = [], []
    for i, plane in enumerate(planes):
        loads.append(pltpu.make_async_copy(strips.at[plane[0], plane[1]], held.at[i], moved.at[i]))
        stores.append(pltpu.make_async_copy(held.at[i], outs[i], moved.at[i]))
    for copy in loads:
        copy.start()
    for load, store in zip(loads, stores):
        load.wait()
        store.start()
    for copy in stores:
        copy.wait()


def place_kernel(peers, waits, ids, positions, *rest):
    own_in, near_in = rest[:2]
    far_ins = rest[2:peers]
    pieces = [own_in, near_in]
    for i in range(0, len(far_ins), 2):
        pieces += [far_ins[i].at[0], far_ins[i + 1]]
    own, rim, ext, got, loaded, stored = rest[peers + waits :]
    rows, cols = own.shape
    blocks = cols // LANES
    size = own_in.shape[-1]
    loads = [
        pltpu.make_async_copy(pieces[offset], got.at[offset], loaded.at[offset]) for offset in range(peers)
    ]
    for copy in loads:
        copy.start()
    flip = reversal(size // 2)
    lane = lax.broadcasted_iota(jnp.int32, (size, LANES), 1)
    ext[...] = jnp.zeros(ext.shape, F32)
    for copy in loads:
        copy.wait()
    fields = mirror_halves([got[offset] for offset in range(peers)], flip)
    for offset in range(peers):
        window = ids[0] ^ offset
        row_first = positions[window, 0] - ids[1] * rows
        col_first = positions[window, 1]
        block_first = col_first >> 7
        within = col_first & (LANES - 1)
        moved = [
            pltpu.roll(fields[offset][:, i * LANES : (i + 1) * LANES], within, 1) for i in range(size // LANES)
        ]
        keep = lane >= within
        zero = jnp.zeros((size, LANES), F32)
        moved = [zero] + moved + [zero]
        for i in range(size // LANES + 1):
            place = (block_first + i, pl.ds(row_first, size))
            ext[place] = ext[place] + jnp.where(keep, moved[i + 1], moved[i])
    stores = []
    for block in range(blocks):
        columns = pl.ds(block * LANES, LANES)
        stores.append(
            pltpu.make_async_copy(ext.at[block, pl.ds(rows, rows)], rim.at[:, columns], stored.at[2 * block])
        )
        stores.append(
            pltpu.make_async_copy(ext.at[block, pl.ds(0, rows)], own.at[:, columns], stored.at[2 * block + 1])
        )
    for copy in stores:
        copy.start()
    for copy in stores:
        copy.wait()


def split_value(x):
    high = x.astype(BF16)
    low = (x - high.astype(F32)).astype(BF16)
    return high, low


def dot32(a, b):
    return jnp.dot(a, b, preferred_element_type=F32)


def sandwich(re, im, tables, base, conj):
    half = re.shape[0] // 2

    def fold(x):
        upper, lower = x[:half], x[half:]
        even, odd = upper + lower, upper - lower
        parts = []
        for y in (even, odd):
            near, far = y[:, :half], y[:, half:]
            parts.append((near + far, near - far))
        return parts

    re_parts, im_parts = fold(re), fold(im)
    middle = []
    for b in range(2):
        field = jnp.concatenate(
            [jnp.concatenate([re_parts[a][b], im_parts[a][b]], axis=1) for a in range(2)], axis=0
        )
        high, low = split_value(field)
        middle.append(
            dot32(high, tables[base + 2 * b + 1 - conj, 0])
            + dot32(low, tables[base + 2 * b + 1 - conj, 0])
            + dot32(high, tables[base + 2 * b + 1 - conj, 1])
        )
    done = []
    for a in range(2):
        rows = slice(a * half, (a + 1) * half)
        field = jnp.concatenate(
            [
                jnp.concatenate([middle[b][rows, :half] for b in range(2)], axis=1),
                jnp.concatenate([middle[b][rows, half:] for b in range(2)], axis=1),
            ],
            axis=0,
        )
        high, low = split_value(field)
        done.append(
            dot32(tables[base + 2 * a + conj, 0], high)
            + dot32(tables[base + 2 * a + conj, 0], low)
            + dot32(tables[base + 2 * a + conj, 1], high)
        )

    def unfold(even, odd):
        rows = jnp.concatenate([even + odd, even - odd], axis=0)
        near, far = rows[:, :half], rows[:, half:]
        return jnp.concatenate([near + far, near - far], axis=1)

    return (
        unfold(done[0][:half], done[1][:half]),
        unfold(done[0][half:], done[1][half:]),
    )


def optics_kernel(peers, per_device, ids, probe_in, amplitude_in, tables_in, tilt_in, *rest):
    chunks = 2 * per_device
    groups = peers // 2 + 1
    crops, pieces = [], []
    for chunk in range(chunks):
        got = rest[chunk * peers : (chunk + 1) * peers]
        crops += list(got[:2])
        for i in range(2, peers, 2):
            crops += [got[i].at[0], got[i + 1]]
    rest = rest[chunks * peers :]
    for chunk in range(chunks):
        out = rest[chunk * groups : (chunk + 1) * groups]
        pieces += list(out[:2])
        for far in out[2:]:
            pieces += [far.at[0], far.at[1]]
    kept, handed = rest[chunks * groups : chunks * groups + 2]
    rest = rest[chunks * groups + 2 :]
    trans, history, terms, grad, tables, tilt, amplitude, fixed, loaded, stored = rest
    size = grad.shape[-1]
    share = size // peers
    layers = peers * per_device
    me = ids[0]
    half = tables.shape[0] // 2
    settings = [
        pltpu.make_async_copy(probe_in, history.at[0], fixed.at[0]),
        pltpu.make_async_copy(tables_in.at[pl.ds(0, half)], tables.at[pl.ds(0, half)], fixed.at[1]),
        pltpu.make_async_copy(tables_in.at[pl.ds(half, half)], tables.at[pl.ds(half, half)], fixed.at[2]),
        pltpu.make_async_copy(tilt_in, tilt, fixed.at[3]),
        pltpu.make_async_copy(amplitude_in, amplitude, fixed.at[4]),
    ]
    for copy in settings[:2]:
        copy.start()
    for j in range(per_device):
        for offset in range(peers):
            at = (me ^ offset) * per_device + j
            for part in range(2):
                pltpu.make_async_copy(
                    crops[(j * 2 + part) * peers + offset], trans.at[at, part], loaded.at[2 * at + part]
                ).start()
    for copy in settings[2:]:
        copy.start()
    for copy in settings[:2]:
        copy.wait()

    def mixed(layer):
        for part in range(2):
            pltpu.make_async_copy(crops[0], trans.at[layer, part], loaded.at[2 * layer + part]).wait()
        t_re, t_im = trans[layer, 0], trans[layer, 1]
        w_re, w_im = history[layer, 0], history[layer, 1]
        return t_re * w_re - t_im * w_im, t_re * w_im + t_im * w_re

    def forward(layer, carry):
        re, im = mixed(layer)
        re, im = sandwich(re, im, tables, 0, 0)
        history[layer + 1, 0] = re
        history[layer + 1, 1] = im
        return carry

    lax.fori_loop(0, layers - 1, forward, 0, unroll=True)
    re, im = mixed(layers - 1)
    for copy in settings[2:]:
        copy.wait()
    d_re, d_im = tilt[0], tilt[1]
    re, im = re * d_re - im * d_im, re * d_im + im * d_re
    re, im = sandwich(re, im, tables, 4, 0)
    factor = 1.0 - amplitude[...] / jnp.sqrt(re * re + im * im + 1.0)
    re, im = sandwich(re * factor, im * factor, tables, 4, 1)
    back_re, back_im = re * d_re + im * d_im, im * d_re - re * d_im

    def collect(layer, back_re, back_im):
        w_re, w_im = history[layer, 0], history[layer, 1]
        terms[layer, 0] = w_re * back_re + w_im * back_im
        terms[layer, 1] = w_re * back_im - w_im * back_re
        owner, j_now = lax.div(layer, per_device), lax.rem(layer, per_device)
        for j in range(per_device):
            for offset in range(peers):

                @pl.when((owner == me ^ offset) & (j_now == j))
                def _():
                    for part in range(2):
                        pltpu.make_async_copy(
                            terms.at[layer, part],
                            pieces[(j * 2 + part) * peers + offset].at[pl.ds(0, size)],
                            stored.at[2 * layer + part],
                        ).start()

        t_re, t_im = trans[layer, 0], trans[layer, 1]
        grad[0] = t_re * back_re + t_im * back_im
        grad[1] = t_re * back_im - t_im * back_re

    collect(layers - 1, back_re, back_im)

    def backward(step, carry):
        back_re, back_im = sandwich(grad[0], grad[1], tables, 0, 1)
        collect(layers - 2 - step, back_re, back_im)
        return carry

    lax.fori_loop(0, layers - 1, backward, 0, unroll=True)
    grad[0], grad[1] = mirror_halves([grad[0], grad[1]], reversal(size // 2))
    shares = []
    for offset in range(peers):
        first = pl.multiple_of((me ^ offset) * share, share)
        for part in range(2):
            shares.append(
                pltpu.make_async_copy(
                    grad.at[part, pl.ds(first, share)],
                    (kept, handed)[offset % 2].at[offset // 2, part],
                    fixed.at[2 * offset + part],
                )
            )
    for copy in shares:
        copy.start()
    for layer in range(layers):
        for part in range(2):
            pltpu.make_async_copy(
                terms.at[layer, part], pieces[0].at[pl.ds(0, size)], stored.at[2 * layer + part]
            ).wait()
    for copy in shares:
        copy.wait()


SMEM_SPEC = pl.BlockSpec(memory_space=pltpu.SMEM)
VMEM_SPEC = pl.BlockSpec(memory_space=pltpu.VMEM)
HBM_SPEC = pl.BlockSpec(memory_space=pltpu.HBM)


def gate_kernel(*refs):
    pass


def gate(passed, waits):
    total = len(passed)
    if not total or not waits:
        return passed
    return run_kernel(
        gate_kernel,
        "gate",
        tuple(shape(*x.shape) for x in passed),
        [HBM_SPEC] * (total + len(waits)),
        (HBM_SPEC,) * total,
        [],
        0.1,
        aliases={i: i for i in range(total)},
    )(*passed, *waits)


def run_kernel(kernel, name, out_shapes, in_specs, out_specs, scratch, micros, mebibytes=16, aliases={}):
    return pl.pallas_call(
        kernel,
        name=name,
        out_shape=out_shapes,
        in_specs=in_specs,
        out_specs=out_specs,
        scratch_shapes=scratch,
        input_output_aliases=aliases,
        compiler_params=pltpu.CompilerParams(vmem_limit_bytes=mebibytes * 2**20),
        cost_estimate=pl.CostEstimate(
            flops=int(micros * 1e6), bytes_accessed=int(micros * 1e3), transcendentals=0
        ),
    )


def shape(*dims):
    return jax.ShapeDtypeStruct(dims, F32)


def swap(x, axis, offset):
    peers = lax.axis_size(axis)
    return lax.ppermute(x, axis, [(i, i ^ offset) for i in range(peers)])


def exchanged(mine, waits=()):
    got = [mine[0], swap(mine[1], "depth", 1)]
    for i, pair in enumerate(mine[2:]):
        across = swap(pair, "depth", 2 * (i + 1))
        (across,) = gate([across], waits)
        got += [across, swap(across[1], "depth", 1)]
    return got


def echo(x):
    return swap(x[:8, :LANES], "depth", 1)


def shift(x, axis, by):
    peers = lax.axis_size(axis)
    return lax.ppermute(x, axis, [(i, i + by) for i in range(peers) if 0 <= i + by < peers])


def body(transmission, probe_field, scan_positions, amplitudes):
    size = probe_field.shape[-1]
    per_device, _, rows, cols = transmission.shape
    peers = lax.axis_size("depth")
    tiles = lax.axis_size("tile")
    ids = jnp.stack([lax.axis_index("depth"), lax.axis_index("tile")]).astype(jnp.int32)
    tables, tilt = (jnp.asarray(x) for x in optics_tables(size))

    probe, amplitude = run_kernel(
        prep_kernel,
        "prep",
        (shape(2, size, size), shape(size, size)),
        [SMEM_SPEC, VMEM_SPEC, VMEM_SPEC],
        [VMEM_SPEC, VMEM_SPEC],
        [],
        2,
    )(ids, probe_field, amplitudes)

    chunks = [(j, part) for j in range(per_device) for part in range(2)]
    ahead = 2

    def strips_of(planes, waits):
        return run_kernel(
            functools.partial(strip_kernel, planes, len(waits)),
            "strip",
            (shape(rows, cols),) * len(planes),
            [HBM_SPEC] * (1 + len(waits)),
            (HBM_SPEC,) * len(planes),
            [pltpu.VMEM((len(planes), rows, cols), F32), pltpu.SemaphoreType.DMA((len(planes),))],
            1,
            56,
        )(transmission, *waits)

    strips = list(strips_of(chunks[:1], []))
    strips += strips_of(chunks[1:], strips[:1])
    strips[1:2] = gate(strips[1:2], [amplitude])
    group = (shape(size, size),) * 2 + (shape(2, size, size),) * (peers // 2 - 1)
    groups = len(group)
    crops = []
    for k, c in enumerate(chunks):
        rim = shift(strips[k], "tile", -1)
        waits = crops[k - ahead][2::2] if k >= ahead else [probe, amplitude]
        mine = run_kernel(
            functools.partial(crop_kernel, peers, c, len(waits)),
            "crop",
            group,
            [SMEM_SPEC, SMEM_SPEC] + [HBM_SPEC] * (2 + len(waits)),
            (HBM_SPEC,) * groups,
            [
                pltpu.VMEM((cols // LANES + 1, 2 * rows, LANES), F32),
                pltpu.VMEM((peers, size, size), F32),
                pltpu.SemaphoreType.DMA((2 * cols // LANES,)),
                pltpu.SemaphoreType.DMA((peers,)),
            ],
            2,
        )(ids, scan_positions, transmission, rim, *waits)
        strips[k + ahead : k + ahead + 1] = gate(strips[k + ahead : k + ahead + 1], mine[:1])
        early = [x for got in crops[:-1] for x in got[1:2] + got[3::2]] if k == len(chunks) - 1 else []
        crops.append(exchanged(mine, early))
    layers = per_device * peers
    result = run_kernel(
        functools.partial(optics_kernel, peers, per_device),
        "optics",
        group * len(chunks) + (shape(peers // 2, 2, size // peers, size),) * 2,
        [SMEM_SPEC] + [HBM_SPEC] * (4 + len(chunks) * peers),
        (HBM_SPEC,) * (len(chunks) * groups + 2),
        [
            pltpu.VMEM((layers, 2, size, size), F32),
            pltpu.VMEM((layers, 2, size, size), F32),
            pltpu.VMEM((layers, 2, size, size), F32),
            pltpu.VMEM((2, size, size), F32),
            pltpu.VMEM(tables.shape, BF16),
            pltpu.VMEM(tilt.shape, F32),
            pltpu.VMEM((size, size), F32),
            pltpu.SemaphoreType.DMA((max(5, 2 * peers),)),
            pltpu.SemaphoreType.DMA((2 * layers,)),
            pltpu.SemaphoreType.DMA((2 * layers,)),
        ],
        15,
        32,
    )(ids, probe, amplitude, tables, tilt, *[x for got in crops for x in got])

    kept, handed = result[-2:]
    probe_halves = kept + swap(handed, "depth", 1)
    probe_grad = probe_halves
    step = 2
    while step < peers:
        probe_grad = probe_grad[:1] + swap(probe_grad[1:], "depth", step)
        step *= 2
    probe_steps = [probe_grad[0]]
    step = tiles // 2
    while step:
        probe_steps.append(probe_steps[-1] + swap(probe_steps[-1], "tile", step))
        step //= 2

    own, rim_back, returned = {}, {}, []
    order = list(reversed(chunks))
    for k, c in enumerate(order):
        at = chunks.index(c) * groups
        mine = result[at : at + groups]
        if k == 0:
            mine = gate(mine, [probe_steps[0]])
        if k >= ahead:
            mine = gate(mine, returned[1][2::2] + [own[order[k - ahead]]])
        before = [own[order[k - 1]]] if k else probe_steps[-2:-1]
        if k == ahead:
            before.append(rim_back[order[k - ahead]])
        returned.append(exchanged(mine, before))
        waits = [swap(swap(probe_steps[-1], "depth", 1), "depth", 1)] if k == 1 else []
        mine = run_kernel(
            functools.partial(place_kernel, peers, len(waits)),
            "place",
            (shape(rows, cols), shape(rows, cols)),
            [SMEM_SPEC, SMEM_SPEC] + [HBM_SPEC] * (peers + len(waits)),
            (HBM_SPEC, HBM_SPEC),
            [
                pltpu.VMEM((cols // LANES + 1, 2 * rows, LANES), F32),
                pltpu.VMEM((peers, size, size), F32),
                pltpu.SemaphoreType.DMA((peers,)),
                pltpu.SemaphoreType.DMA((2 * cols // LANES,)),
            ],
            2,
        )(ids, scan_positions, *returned[k], *waits)
        own[c], outside = mine[:2]
        if k >= ahead:
            earlier = order[k - ahead]
            (rim_back[earlier],) = gate([rim_back[earlier]], [own[order[k - 1]]])
            (outside,) = gate([outside], [echo(echo(rim_back[order[k - ahead]]))])
        rim_back[c] = shift(outside, "tile", 1)

    rim_back[order[-2]] = gate([rim_back[order[-2]]], [swap(rim_back[order[-2]][: rows // 2], "depth", 1)])[0]
    object_grad = jnp.stack(
        [
            jnp.stack([own[(j, part)] + rim_back[(j, part)] for part in range(2)])
            for j in range(per_device)
        ]
    )
    return (object_grad, probe_steps[-1])


def solution(mesh):
    placed = (P("depth", None, "tile", None), P(), P("tile", None), P("tile", None, None))
    return jax.shard_map(
        body,
        mesh=mesh,
        in_specs=placed,
        out_specs=(P("depth", None, "tile", None), P(None, "depth", None)),
        check_vma=False,
    )
```

```python
import functools

import jax
import jax.numpy as jnp
import ml_dtypes
import numpy as np
from jax import lax
from jax.experimental import pallas as pl
from jax.experimental.pallas import tpu as pltpu
from jax.sharding import PartitionSpec as P

LANES = 128
F32 = jnp.float32
BF16 = jnp.bfloat16


def split_table(table):
    high = table.astype(np.float32).astype(ml_dtypes.bfloat16)
    low = (table - high.astype(np.float64)).astype(np.float32).astype(ml_dtypes.bfloat16)
    return high, low


def left_form(matrix):
    return np.block([[matrix.real, -matrix.imag], [matrix.imag, matrix.real]])


def folded(matrix):
    half = matrix.shape[0] // 2
    near = matrix[:half, :half]
    mirrored = matrix[:half, half:][:, ::-1]
    return (near + mirrored) / 2, (near - mirrored) / 2


def optics_tables(length):
    index = np.arange(length)
    fourier = np.exp(-2j * np.pi * (index[:, None] * index[None, :] % length) / length)
    frequency = np.where(index < length // 2, index, index - length).astype(np.float64)
    phase = np.exp(-1j * np.pi * frequency**2 / (4 * length))
    fresnel = (np.conj(fourier) * phase[None, :]) @ fourier / length
    odd = 2 * index + 1
    turn = odd[:, None] * odd[None, :] % (4 * length)
    shifted = np.exp(-2j * np.pi * turn / (4 * length)) / np.sqrt(length)
    tables = []
    for matrix in (fresnel, shifted):
        for block in folded(matrix):
            for form in (left_form(block), left_form(np.conj(block))):
                tables.append(np.stack(split_table(form)))
    order = np.concatenate([index[: length // 2], index[length // 2 :][::-1]])
    ramp = np.exp(1j * np.pi * order / length)
    tilt = ramp[:, None] * ramp[None, :]
    return np.stack(tables), np.stack([tilt.real, tilt.imag]).astype(np.float32)


def reversal(size):
    row = lax.broadcasted_iota(jnp.int32, (size, size), 0)
    col = lax.broadcasted_iota(jnp.int32, (size, size), 1)
    return jnp.where(row + col == size - 1, 1.0, 0.0).astype(BF16)


def exact_dot(a, b):
    moving, table = (a, b) if b.dtype == BF16 else (b, a)
    total = None
    for part in range(3):
        piece = moving.astype(BF16)
        moving = moving - piece.astype(F32)
        done = jnp.dot(*((piece, b) if b.dtype == BF16 else (a, piece)), preferred_element_type=F32)
        total = done if total is None else total + done
    return total


def mirror_halves(fields, flip):
    count, size = len(fields), fields[0].shape[0]
    half = size // 2
    right = exact_dot(jnp.concatenate([x[:, half:] for x in fields], axis=0), flip)
    fields = [
        jnp.concatenate([x[:, :half], right[i * size : (i + 1) * size]], axis=1) for i, x in enumerate(fields)
    ]
    lower = exact_dot(flip, jnp.concatenate([x[half:] for x in fields], axis=1))
    return [
        jnp.concatenate([x[:half], lower[:, i * size : (i + 1) * size]], axis=0) for i, x in enumerate(fields)
    ]


def prep_kernel(ids, probe, amplitudes, probe_out, amp_out):
    flip = reversal(probe.shape[-1] // 2)
    probe_out[0], probe_out[1], amp_out[...] = mirror_halves([probe[0], probe[1], amplitudes[ids[0]]], flip)


def crop_kernel(peers, waits, ids, positions, strip, rim, *rest):
    rest = rest[waits:]
    own_out, near_out = rest[:2]
    far_outs, rest = rest[2 : peers // 2 + 1], rest[peers // 2 + 1 :]
    outs = [own_out, near_out] + [far.at[i] for far in far_outs for i in range(2)]
    ext, cut, loaded, stored = rest
    rows, cols = rim.shape
    blocks = cols // LANES
    size = own_out.shape[-1]
    loads = []
    for block in range(blocks):
        columns = pl.ds(block * LANES, LANES)
        loads.append(
            pltpu.make_async_copy(
                strip.at[:, columns], ext.at[block, pl.ds(0, rows)], loaded.at[2 * block]
            )
        )
        loads.append(
            pltpu.make_async_copy(
                rim.at[:, columns], ext.at[block, pl.ds(rows, rows)], loaded.at[2 * block + 1]
            )
        )
    for copy in loads:
        copy.start()
    flip = reversal(size // 2)
    lane = lax.broadcasted_iota(jnp.int32, (size, LANES), 1)
    ext[blocks] = jnp.zeros((2 * rows, LANES), F32)
    for copy in loads:
        copy.wait()
    stores = []
    for pair in sorted(range(0, peers, 2), reverse=True):
        fields = []
        for offset in (pair, pair + 1):
            window = ids[0] ^ offset
            row_first = positions[window, 0] - ids[1] * rows
            col_first = positions[window, 1]
            block_first = col_first >> 7
            within = col_first & (LANES - 1)
            moved = [
                pltpu.roll(
                    ext[block_first + i, pl.ds(row_first, size), :], (LANES - within) & (LANES - 1), 1
                )
                for i in range(size // LANES + 1)
            ]
            keep = lane < LANES - within
            picked = [jnp.where(keep, moved[i], moved[i + 1]) for i in range(size // LANES)]
            fields.append(jnp.concatenate(picked, axis=1))
        fields = mirror_halves(fields, flip)
        for i, offset in enumerate((pair, pair + 1)):
            cut[offset] = fields[i]
            copy = pltpu.make_async_copy(cut.at[offset], outs[offset], stored.at[offset])
            copy.start()
            stores.append(copy)
    for copy in stores:
        copy.wait()


def strip_kernel(planes, waits, strips, *rest):
    outs = rest[waits : waits + len(planes)]
    held, moved = rest[waits + len(planes) :]
    loads, stores = [], []
    for i, plane in enumerate(planes):
        loads.append(pltpu.make_async_copy(strips.at[plane[0], plane[1]], held.at[i], moved.at[i]))
        stores.append(pltpu.make_async_copy(held.at[i], outs[i], moved.at[i]))
    for copy in loads:
        copy.start()
    for load, store in zip(loads, stores):
        load.wait()
        store.start()
    for copy in stores:
        copy.wait()


def place_kernel(peers, waits, ids, positions, *rest):
    own_in, near_in = rest[:2]
    far_ins = rest[2:peers]
    pieces = [own_in, near_in]
    for i in range(0, len(far_ins), 2):
        pieces += [far_ins[i].at[0], far_ins[i + 1]]
    own, rim, ext, got, loaded, stored = rest[peers + waits :]
    rows, cols = own.shape
    blocks = cols // LANES
    size = own_in.shape[-1]
    loads = [
        pltpu.make_async_copy(pieces[offset], got.at[offset], loaded.at[offset]) for offset in range(peers)
    ]
    for copy in loads:
        copy.start()
    flip = reversal(size // 2)
    lane = lax.broadcasted_iota(jnp.int32, (size, LANES), 1)
    ext[...] = jnp.zeros(ext.shape, F32)
    for copy in loads:
        copy.wait()
    fields = mirror_halves([got[offset] for offset in range(peers)], flip)
    for offset in range(peers):
        window = ids[0] ^ offset
        row_first = positions[window, 0] - ids[1] * rows
        col_first = positions[window, 1]
        block_first = col_first >> 7
        within = col_first & (LANES - 1)
        moved = [
            pltpu.roll(fields[offset][:, i * LANES : (i + 1) * LANES], within, 1) for i in range(size // LANES)
        ]
        keep = lane >= within
        zero = jnp.zeros((size, LANES), F32)
        moved = [zero] + moved + [zero]
        for i in range(size // LANES + 1):
            place = (block_first + i, pl.ds(row_first, size))
            ext[place] = ext[place] + jnp.where(keep, moved[i + 1], moved[i])
    stores = []
    for block in range(blocks):
        columns = pl.ds(block * LANES, LANES)
        stores.append(
            pltpu.make_async_copy(ext.at[block, pl.ds(rows, rows)], rim.at[:, columns], stored.at[2 * block])
        )
        stores.append(
            pltpu.make_async_copy(ext.at[block, pl.ds(0, rows)], own.at[:, columns], stored.at[2 * block + 1])
        )
    for copy in stores:
        copy.start()
    for copy in stores:
        copy.wait()


def split_value(x):
    high = x.astype(BF16)
    low = (x - high.astype(F32)).astype(BF16)
    return high, low


def dot32(a, b):
    return jnp.dot(a, b, preferred_element_type=F32)


def sandwich(re, im, tables, base, conj):
    half = re.shape[0] // 2

    def fold(x):
        upper, lower = x[:half], x[half:]
        even, odd = upper + lower, upper - lower
        parts = []
        for y in (even, odd):
            near, far = y[:, :half], y[:, half:]
            parts.append((near + far, near - far))
        return parts

    re_parts, im_parts = fold(re), fold(im)
    middle = []
    for b in range(2):
        field = jnp.concatenate(
            [jnp.concatenate([re_parts[a][b], im_parts[a][b]], axis=1) for a in range(2)], axis=0
        )
        high, low = split_value(field)
        middle.append(
            dot32(high, tables[base + 2 * b + 1 - conj, 0])
            + dot32(low, tables[base + 2 * b + 1 - conj, 0])
            + dot32(high, tables[base + 2 * b + 1 - conj, 1])
        )
    done = []
    for a in range(2):
        rows = slice(a * half, (a + 1) * half)
        field = jnp.concatenate(
            [
                jnp.concatenate([middle[b][rows, :half] for b in range(2)], axis=1),
                jnp.concatenate([middle[b][rows, half:] for b in range(2)], axis=1),
            ],
            axis=0,
        )
        high, low = split_value(field)
        done.append(
            dot32(tables[base + 2 * a + conj, 0], high)
            + dot32(tables[base + 2 * a + conj, 0], low)
            + dot32(tables[base + 2 * a + conj, 1], high)
        )

    def unfold(even, odd):
        rows = jnp.concatenate([even + odd, even - odd], axis=0)
        near, far = rows[:, :half], rows[:, half:]
        return jnp.concatenate([near + far, near - far], axis=1)

    return (
        unfold(done[0][:half], done[1][:half]),
        unfold(done[0][half:], done[1][half:]),
    )


def optics_kernel(peers, per_device, ids, probe_in, amplitude_in, tables_in, tilt_in, *rest):
    chunks = 2 * per_device
    groups = peers // 2 + 1
    crops, pieces = [], []
    for chunk in range(chunks):
        got = rest[chunk * peers : (chunk + 1) * peers]
        crops += list(got[:2])
        for i in range(2, peers, 2):
            crops += [got[i].at[0], got[i + 1]]
    rest = rest[chunks * peers :]
    for chunk in range(chunks):
        out = rest[chunk * groups : (chunk + 1) * groups]
        pieces += list(out[:2])
        for far in out[2:]:
            pieces += [far.at[0], far.at[1]]
    kept, handed = rest[chunks * groups : chunks * groups + 2]
    rest = rest[chunks * groups + 2 :]
    trans, history, terms, grad, tables, tilt, amplitude, fixed, loaded, stored = rest
    size = grad.shape[-1]
    share = size // peers
    layers = peers * per_device
    me = ids[0]
    half = tables.shape[0] // 2
    settings = [
        pltpu.make_async_copy(probe_in, history.at[0], fixed.at[0]),
        pltpu.make_async_copy(tables_in.at[pl.ds(0, half)], tables.at[pl.ds(0, half)], fixed.at[1]),
        pltpu.make_async_copy(tables_in.at[pl.ds(half, half)], tables.at[pl.ds(half, half)], fixed.at[2]),
        pltpu.make_async_copy(tilt_in, tilt, fixed.at[3]),
        pltpu.make_async_copy(amplitude_in, amplitude, fixed.at[4]),
    ]
    for copy in settings[:2]:
        copy.start()
    for j in range(per_device):
        for offset in range(peers):
            at = (me ^ offset) * per_device + j
            for part in range(2):
                pltpu.make_async_copy(
                    crops[(j * 2 + part) * peers + offset], trans.at[at, part], loaded.at[2 * at + part]
                ).start()
    for copy in settings[2:]:
        copy.start()
    for copy in settings[:2]:
        copy.wait()

    def mixed(layer):
        for part in range(2):
            pltpu.make_async_copy(crops[0], trans.at[layer, part], loaded.at[2 * layer + part]).wait()
        t_re, t_im = trans[layer, 0], trans[layer, 1]
        w_re, w_im = history[layer, 0], history[layer, 1]
        return t_re * w_re - t_im * w_im, t_re * w_im + t_im * w_re

    def forward(layer, carry):
        re, im = mixed(layer)
        re, im = sandwich(re, im, tables, 0, 0)
        history[layer + 1, 0] = re
        history[layer + 1, 1] = im
        return carry

    lax.fori_loop(0, layers - 1, forward, 0, unroll=True)
    re, im = mixed(layers - 1)
    for copy in settings[2:]:
        copy.wait()
    d_re, d_im = tilt[0], tilt[1]
    re, im = re * d_re - im * d_im, re * d_im + im * d_re
    re, im = sandwich(re, im, tables, 4, 0)
    factor = 1.0 - amplitude[...] / jnp.sqrt(re * re + im * im + 1.0)
    re, im = sandwich(re * factor, im * factor, tables, 4, 1)
    back_re, back_im = re * d_re + im * d_im, im * d_re - re * d_im

    def collect(layer, back_re, back_im):
        w_re, w_im = history[layer, 0], history[layer, 1]
        terms[layer, 0] = w_re * back_re + w_im * back_im
        terms[layer, 1] = w_re * back_im - w_im * back_re
        owner, j_now = lax.div(layer, per_device), lax.rem(layer, per_device)
        for j in range(per_device):
            for offset in range(peers):

                @pl.when((owner == me ^ offset) & (j_now == j))
                def _():
                    for part in range(2):
                        pltpu.make_async_copy(
                            terms.at[layer, part],
                            pieces[(j * 2 + part) * peers + offset].at[pl.ds(0, size)],
                            stored.at[2 * layer + part],
                        ).start()

        t_re, t_im = trans[layer, 0], trans[layer, 1]
        grad[0] = t_re * back_re + t_im * back_im
        grad[1] = t_re * back_im - t_im * back_re

    collect(layers - 1, back_re, back_im)

    def backward(step, carry):
        back_re, back_im = sandwich(grad[0], grad[1], tables, 0, 1)
        collect(layers - 2 - step, back_re, back_im)
        return carry

    lax.fori_loop(0, layers - 1, backward, 0, unroll=True)
    grad[0], grad[1] = mirror_halves([grad[0], grad[1]], reversal(size // 2))
    shares = []
    for offset in range(peers):
        first = pl.multiple_of((me ^ offset) * share, share)
        for part in range(2):
            shares.append(
                pltpu.make_async_copy(
                    grad.at[part, pl.ds(first, share)],
                    (kept, handed)[offset % 2].at[offset // 2, part],
                    fixed.at[2 * offset + part],
                )
            )
    for copy in shares:
        copy.start()
    for layer in range(layers):
        for part in range(2):
            pltpu.make_async_copy(
                terms.at[layer, part], pieces[0].at[pl.ds(0, size)], stored.at[2 * layer + part]
            ).wait()
    for copy in shares:
        copy.wait()


SMEM_SPEC = pl.BlockSpec(memory_space=pltpu.SMEM)
VMEM_SPEC = pl.BlockSpec(memory_space=pltpu.VMEM)
HBM_SPEC = pl.BlockSpec(memory_space=pltpu.HBM)


def gate_kernel(*refs):
    pass


def gate(passed, waits):
    total = len(passed)
    if not total or not waits:
        return passed
    return run_kernel(
        gate_kernel,
        "gate",
        tuple(shape(*x.shape) for x in passed),
        [HBM_SPEC] * (total + len(waits)),
        (HBM_SPEC,) * total,
        [],
        0.1,
        aliases={i: i for i in range(total)},
    )(*passed, *waits)


def run_kernel(kernel, name, out_shapes, in_specs, out_specs, scratch, micros, mebibytes=16, aliases={}):
    return pl.pallas_call(
        kernel,
        name=name,
        out_shape=out_shapes,
        in_specs=in_specs,
        out_specs=out_specs,
        scratch_shapes=scratch,
        input_output_aliases=aliases,
        compiler_params=pltpu.CompilerParams(vmem_limit_bytes=mebibytes * 2**20),
        cost_estimate=pl.CostEstimate(
            flops=int(micros * 1e6), bytes_accessed=int(micros * 1e3), transcendentals=0
        ),
    )


def shape(*dims):
    return jax.ShapeDtypeStruct(dims, F32)


def swap(x, axis, offset):
    peers = lax.axis_size(axis)
    return lax.ppermute(x, axis, [(i, i ^ offset) for i in range(peers)])


def exchanged(mine, waits=()):
    got = [mine[0], swap(mine[1], "depth", 1)]
    for i, pair in enumerate(mine[2:]):
        across = swap(pair, "depth", 2 * (i + 1))
        (across,) = gate([across], waits)
        got += [across, swap(across[1], "depth", 1)]
    return got


def echo(x):
    return swap(x[:8, :LANES], "depth", 1)


def shift(x, axis, by):
    peers = lax.axis_size(axis)
    return lax.ppermute(x, axis, [(i, i + by) for i in range(peers) if 0 <= i + by < peers])


def body(transmission, probe_field, scan_positions, amplitudes):
    size = probe_field.shape[-1]
    per_device, _, rows, cols = transmission.shape
    peers = lax.axis_size("depth")
    tiles = lax.axis_size("tile")
    ids = jnp.stack([lax.axis_index("depth"), lax.axis_index("tile")]).astype(jnp.int32)
    tables, tilt = (jnp.asarray(x) for x in optics_tables(size))

    probe, amplitude = run_kernel(
        prep_kernel,
        "prep",
        (shape(2, size, size), shape(size, size)),
        [SMEM_SPEC, VMEM_SPEC, VMEM_SPEC],
        [VMEM_SPEC, VMEM_SPEC],
        [],
        2,
    )(ids, probe_field, amplitudes)

    chunks = [(j, part) for j in range(per_device) for part in range(2)]
    ahead = 2

    def strips_of(planes, waits):
        return run_kernel(
            functools.partial(strip_kernel, planes, len(waits)),
            "strip",
            (shape(rows, cols),) * len(planes),
            [HBM_SPEC] * (1 + len(waits)),
            (HBM_SPEC,) * len(planes),
            [pltpu.VMEM((len(planes), rows, cols), F32), pltpu.SemaphoreType.DMA((len(planes),))],
            1,
            56,
        )(transmission, *waits)

    strips = list(strips_of(chunks[:1], []))
    strips += strips_of(chunks[1:], strips[:1])
    strips[1:2] = gate(strips[1:2], [amplitude])
    group = (shape(size, size),) * 2 + (shape(2, size, size),) * (peers // 2 - 1)
    groups = len(group)
    crops = []
    for k, c in enumerate(chunks):
        rim = shift(strips[k], "tile", -1)
        waits = crops[k - ahead][2::2] if k >= ahead else [probe, amplitude]
        mine = run_kernel(
            functools.partial(crop_kernel, peers, len(waits)),
            "crop",
            group,
            [SMEM_SPEC, SMEM_SPEC] + [HBM_SPEC] * (2 + len(waits)),
            (HBM_SPEC,) * groups,
            [
                pltpu.VMEM((cols // LANES + 1, 2 * rows, LANES), F32),
                pltpu.VMEM((peers, size, size), F32),
                pltpu.SemaphoreType.DMA((2 * cols // LANES,)),
                pltpu.SemaphoreType.DMA((peers,)),
            ],
            2,
        )(ids, scan_positions, strips[k], rim, *waits)
        strips[k + ahead : k + ahead + 1] = gate(strips[k + ahead : k + ahead + 1], mine[:1])
        early = [x for got in crops[:-1] for x in got[1:2] + got[3::2]] if k == len(chunks) - 1 else []
        crops.append(exchanged(mine, early))
    layers = per_device * peers
    result = run_kernel(
        functools.partial(optics_kernel, peers, per_device),
        "optics",
        group * len(chunks) + (shape(peers // 2, 2, size // peers, size),) * 2,
        [SMEM_SPEC] + [HBM_SPEC] * (4 + len(chunks) * peers),
        (HBM_SPEC,) * (len(chunks) * groups + 2),
        [
            pltpu.VMEM((layers, 2, size, size), F32),
            pltpu.VMEM((layers, 2, size, size), F32),
            pltpu.VMEM((layers, 2, size, size), F32),
            pltpu.VMEM((2, size, size), F32),
            pltpu.VMEM(tables.shape, BF16),
            pltpu.VMEM(tilt.shape, F32),
            pltpu.VMEM((size, size), F32),
            pltpu.SemaphoreType.DMA((max(5, 2 * peers),)),
            pltpu.SemaphoreType.DMA((2 * layers,)),
            pltpu.SemaphoreType.DMA((2 * layers,)),
        ],
        15,
        32,
    )(ids, probe, amplitude, tables, tilt, *[x for got in crops for x in got])

    kept, handed = result[-2:]
    probe_halves = kept + swap(handed, "depth", 1)
    probe_grad = probe_halves
    step = 2
    while step < peers:
        probe_grad = probe_grad[:1] + swap(probe_grad[1:], "depth", step)
        step *= 2
    probe_steps = [probe_grad[0]]
    step = tiles // 2
    while step:
        probe_steps.append(probe_steps[-1] + swap(probe_steps[-1], "tile", step))
        step //= 2

    own, rim_back, returned = {}, {}, []
    order = list(reversed(chunks))
    for k, c in enumerate(order):
        at = chunks.index(c) * groups
        mine = result[at : at + groups]
        if k == 0:
            mine = gate(mine, [probe_steps[0]])
        if k >= ahead:
            mine = gate(mine, returned[1][2::2] + [own[order[k - ahead]]])
        before = [own[order[k - 1]]] if k else probe_steps[-2:-1]
        if k == ahead:
            before.append(rim_back[order[k - ahead]])
        returned.append(exchanged(mine, before))
        waits = [swap(swap(probe_steps[-1], "depth", 1), "depth", 1)] if k == 1 else []
        mine = run_kernel(
            functools.partial(place_kernel, peers, len(waits)),
            "place",
            (shape(rows, cols), shape(rows, cols)),
            [SMEM_SPEC, SMEM_SPEC] + [HBM_SPEC] * (peers + len(waits)),
            (HBM_SPEC, HBM_SPEC),
            [
                pltpu.VMEM((cols // LANES + 1, 2 * rows, LANES), F32),
                pltpu.VMEM((peers, size, size), F32),
                pltpu.SemaphoreType.DMA((peers,)),
                pltpu.SemaphoreType.DMA((2 * cols // LANES,)),
            ],
            2,
        )(ids, scan_positions, *returned[k], *waits)
        own[c], outside = mine[:2]
        if k >= ahead:
            earlier = order[k - ahead]
            (rim_back[earlier],) = gate([rim_back[earlier]], [own[order[k - 1]]])
            (outside,) = gate([outside], [echo(echo(rim_back[order[k - ahead]]))])
        rim_back[c] = shift(outside, "tile", 1)

    rim_back[order[-2]] = gate([rim_back[order[-2]]], [swap(rim_back[order[-2]][: rows // 2], "depth", 1)])[0]
    object_grad = jnp.stack(
        [
            jnp.stack([own[(j, part)] + rim_back[(j, part)] for part in range(2)])
            for j in range(per_device)
        ]
    )
    return (object_grad, probe_steps[-1])


def solution(mesh):
    placed = (P("depth", None, "tile", None), P(), P("tile", None), P("tile", None, None))
    return jax.shard_map(
        body,
        mesh=mesh,
        in_specs=placed,
        out_specs=(P("depth", None, "tile", None), P(None, "depth", None)),
        check_vma=False,
    )
```
